512 devices in a mesh: blk: 16 (over z_hi, y), grp: 32 (over x, z_lo, core).
Axes of the slice: x: 4, y: 8, z: 8 (z_hi: 2, z_lo: 4; z = z_hi * 4 + z_lo), core: 2. Of those that a mesh axis runs over, the one named last changes fastest.
Arguments:
- matrix: bfloat16 [8192, 8192], P('blk', 'grp'), as said below
- in_pattern: int32 [64, 64], P('blk', 'grp'), may hold values from 0 to 1, as said below
- out_pattern: int32 [64, 64], P('blk', 'grp'), may hold values from 0 to 1, as said below
Outputs:
- pruned: bfloat16 [8192, 8192], P('blk', 'grp')
The draws below stay inside these ranges and needn't reach their ends.
Inputs may be any that keep to these rules, and one draw needn't show every extreme that they name: `matrix`: entries are positive. `in_pattern`: every diagonal tile is present. In the 4 x 2 block of tiles of rows [b * 4, (b + 1) * 4) and columns [g * 2, (g + 1) * 2), for every b and g, at most 4 tiles are present, and some such block holds exactly 4. `out_pattern`: every diagonal tile is kept.
All inputs are finite; a program needn't handle non-finite values.
Results may differ from the reference program's by a relative error of at most 0.001.
Values may be sent and summed in bfloat16 or wider, within the bound.
No kernel may reach another device: no remote copies, remote signals or barrier semaphores. Data moves between devices by JAX's collectives and lax.ppermute only.
A program may use at most 64 MiB of HBM per device.

```python
import math
import jax
import jax.numpy as jnp

TILE = 128
RB = 4
NB = 64
CB = 2


def draw_matrix(key, part):
    key = jax.random.fold_in(key, 1)
    rows = NB * TILE
    place = jnp.arange(rows, dtype=jnp.float32) / float(rows)
    key_a = jax.random.fold_in(key, 0)
    spread = jnp.clip(jax.random.normal(key_a, (rows, rows), jnp.float32), -3.0, 3.0)
    row_scale = jnp.exp(math.log(3.0) * place)
    values = jnp.exp(spread) * row_scale[:, None]
    return values.astype(jnp.bfloat16)


def draw_in_pattern(key, part):
    key = jax.random.fold_in(key, 2)
    bands = NB // RB
    panels = NB // CB
    count = RB * CB
    capacity = max(1, count // 2)
    key_a, key_b, key_c = jax.random.split(key, 3)
    tile_row = jnp.arange(NB, dtype=jnp.int32)
    diagonal = (tile_row[:, None] == tile_row[None, :]).astype(jnp.int32)
    noise = jax.random.randint(key_a, (NB, NB), 0, 1 << 16)
    local_index = (tile_row % RB)[:, None] * CB + (tile_row % CB)[None, :]
    score = (noise * count + local_index) * (1 - diagonal) - diagonal
    blocked = score.reshape(bands, RB, panels, CB).transpose(0, 2, 1, 3).reshape(bands, panels, count)
    diag_blocked = diagonal.reshape(bands, RB, panels, CB).transpose(0, 2, 1, 3).reshape(bands, panels, count)
    order_rank = jnp.sum((blocked[:, :, None, :] < blocked[:, :, :, None]).astype(jnp.int32), axis=3)
    wanted = jax.random.randint(key_b, (bands, panels), 1, capacity + 1)
    chosen = jax.random.randint(key_c, (), 0, bands * panels)
    flat_index = jnp.arange(bands * panels, dtype=jnp.int32).reshape(bands, panels)
    wanted = jnp.where(flat_index == chosen, capacity, wanted)
    wanted = jnp.maximum(wanted, jnp.sum(diag_blocked, axis=2))
    present = (order_rank < wanted[:, :, None]).astype(jnp.int32)
    return present.reshape(bands, panels, RB, CB).transpose(0, 2, 1, 3).reshape(NB, NB)


def draw_out_pattern(key, part):
    key = jax.random.fold_in(key, 3)
    picks = jax.random.randint(key, (NB, NB), 0, 2)
    diagonal = jnp.arange(NB, dtype=jnp.int32)[:, None] == jnp.arange(NB, dtype=jnp.int32)[None, :]
    return jnp.logical_or(picks == 1, diagonal).astype(jnp.int32)


def setup_inputs(seed: int = 0) -> dict:
    keys = jax.random.split(jax.random.key(seed), 4)
    matrix = draw_matrix(jax.random.fold_in(keys[3], 71), 0)
    in_pattern = draw_in_pattern(jax.random.fold_in(keys[3], 71), 0)
    out_pattern = draw_out_pattern(jax.random.fold_in(keys[3], 71), 0)
    return {"matrix": matrix, "in_pattern": in_pattern, "out_pattern": out_pattern}


prune_level = 0.5


def apply_mask(values, pattern, dtype):
    rows_t, cols_t = pattern.shape
    tile = values.shape[0] // rows_t
    shaped = values.reshape(rows_t, tile, cols_t, tile) * pattern[:, None, :, None].astype(dtype)
    return shaped.reshape(values.shape)


def reference(matrix, in_pattern, out_pattern):
    masked = apply_mask(matrix, in_pattern, jnp.bfloat16)
    expanded = jnp.dot(masked, masked, preferred_element_type=jnp.float32)
    kept = apply_mask(expanded, out_pattern, jnp.float32)
    inflated = kept * kept
    column_totals = jnp.sum(inflated, axis=0)
    scaled = inflated / column_totals[None, :] * float(NB * TILE)
    return jnp.maximum(scaled - prune_level, 0.0).astype(jnp.bfloat16)
```

```python
import functools

import jax
import jax.numpy as jnp
from jax import lax
from jax.experimental import pallas as pl
from jax.experimental.pallas import tpu as pltpu
from jax.sharding import Mesh, PartitionSpec as P

prune_level = 0.5
TILE = 128
RB = 4
CB = 2
CAP = 4
META = 16
PACK = CAP * TILE + META
AXES = ("zh", "y", "x", "zl", "core")
SIZES = (2, 8, 4, 4, 2)
BLK = ("zh", "y")
GRP = ("x", "zl", "core")


def pack_kernel(pattern, matrix, out):
    count = jnp.int32(0)
    lane = lax.broadcasted_iota(jnp.int32, (META, TILE), 1)
    slots = jnp.full((META, TILE), CAP, jnp.int32)
    for t in range(RB * CB):
        r, s = divmod(t, CB)
        present = pattern[r, s] != 0
        slot = jnp.minimum(count, CAP - 1)

        @pl.when(present)
        def _():
            place = pl.multiple_of(slot * TILE, TILE)
            out[pl.ds(place, TILE), :] = matrix[r * TILE:(r + 1) * TILE, s * TILE:(s + 1) * TILE]

        slots = jnp.where((lane == t) & present, slot, slots)
        count = count + present.astype(jnp.int32)
    out[CAP * TILE:PACK, :] = slots.astype(jnp.float32).astype(jnp.bfloat16)


def pack(matrix, pattern):
    return pl.pallas_call(
        pack_kernel,
        out_shape=jax.ShapeDtypeStruct((PACK, TILE), jnp.bfloat16),
        in_specs=[pl.BlockSpec(memory_space=pltpu.SMEM), pl.BlockSpec(memory_space=pltpu.VMEM)],
        out_specs=pl.BlockSpec(memory_space=pltpu.VMEM),
        name="pack_tiles",
    )(pattern, matrix)


def product_kernel(steps, place, keep, band, *rest):
    panels = rest[:steps]
    out, totals = rest[steps:steps + 2]
    meta, table, sem, a_dense, b_dense, acc = rest[steps + 2:]
    chips = band.shape[0] // CB
    for g in range(CB * chips):
        row = band[g, CAP * TILE:PACK, :].astype(jnp.float32).astype(jnp.int32)
        meta[g:g + 1, :] = row[0:1]
    for j in range(steps):
        for z in range(2):
            row = panels[j][z, CAP * TILE:PACK, :].astype(jnp.float32).astype(jnp.int32)
            at = CB * chips + 2 * j + z
            meta[at:at + 1, :] = row[0:1]
    copy = pltpu.make_async_copy(meta, table, sem)
    copy.start()
    acc[...] = jnp.zeros_like(acc)
    copy.wait()
    y = place[0]

    def spread(ref, index, row, dense, col):
        for t in range(RB * CB):
            r, s = divmod(t, CB)
            slot = table[row, t]
            start = pl.multiple_of(jnp.minimum(slot, CAP - 1) * TILE, TILE)
            tile = ref[index, pl.ds(start, TILE), :]
            tile = jnp.where(slot < CAP, tile, jnp.zeros_like(tile))
            dense[r * TILE:(r + 1) * TILE, col + s * TILE:col + (s + 1) * TILE] = tile

    for j in range(steps):
        source = lax.rem(y - j + steps, steps)
        for z in range(2):
            chip = z * steps + source
            slot = (2 * j + z) % 2
            for c in range(CB):
                g = chip * CB + c
                spread(band, g, g, a_dense.at[slot], c * CB * TILE)
            spread(panels[j], z, CB * chips + 2 * j + z, b_dense.at[slot], 0)
            acc[...] += jnp.dot(a_dense[slot], b_dense[slot], preferred_element_type=jnp.float32)

    for s in range(CB):
        total = jnp.zeros((1, TILE), jnp.float32)
        for r in range(RB):
            at = (slice(r * TILE, (r + 1) * TILE), slice(s * TILE, (s + 1) * TILE))
            kept = acc[at] * keep[r, s].astype(jnp.float32)
            inflated = kept * kept
            out[at] = inflated
            total = total + jnp.sum(inflated, axis=0, keepdims=True)
        totals[:, s * TILE:(s + 1) * TILE] = total


def product(place, keep, band, panels):
    steps = len(panels)
    smem = pl.BlockSpec(memory_space=pltpu.SMEM)
    vmem = pl.BlockSpec(memory_space=pltpu.VMEM)
    entries = band.shape[0] + 2 * steps
    return pl.pallas_call(
        functools.partial(product_kernel, steps),
        out_shape=(
            jax.ShapeDtypeStruct((RB * TILE, CB * TILE), jnp.float32),
            jax.ShapeDtypeStruct((1, CB * TILE), jnp.float32),
        ),
        in_specs=[smem, smem, vmem] + [vmem] * steps,
        out_specs=(vmem, vmem),
        scratch_shapes=[
            pltpu.VMEM((entries, TILE), jnp.int32),
            pltpu.SMEM((entries, TILE), jnp.int32),
            pltpu.SemaphoreType.DMA,
            pltpu.VMEM((2, RB * TILE, RB * TILE), jnp.bfloat16),
            pltpu.VMEM((2, RB * TILE, CB * TILE), jnp.bfloat16),
            pltpu.VMEM((RB * TILE, CB * TILE), jnp.float32),
        ],
        compiler_params=pltpu.CompilerParams(vmem_limit_bytes=40 * 2**20),
        name="product",
    )(place, keep, band, *panels)


def shifted(array, axis, by):
    n = lax.axis_size(axis)
    return lax.ppermute(array, axis, [(i, (i + by) % n) for i in range(n)])


def body(matrix, in_pattern, out_pattern):
    packed = pack(matrix, in_pattern)
    band = lax.all_gather(packed, GRP)
    other = shifted(packed, "zh", 1)
    hi = lax.axis_index("zh")
    own = jnp.where(hi == 0, jnp.stack([packed, other]), jnp.stack([other, packed]))
    steps = lax.axis_size("y")
    up, down = [own], [own]
    for i in range(steps // 2):
        up.append(shifted(up[-1], "y", 1))
        if i < steps // 2 - 1:
            down.append(shifted(down[-1], "y", -1))
    panels = [own] + up[1:] + down[:0:-1]
    place = lax.axis_index("y").reshape(1)
    inflated, totals = product(place, out_pattern, band, panels)
    column_totals = lax.psum(lax.psum(totals, "zh"), "y")
    scaled = inflated / column_totals * float(SIZES[0] * SIZES[1] * RB * TILE)
    return jnp.maximum(scaled - prune_level, 0.0).astype(jnp.bfloat16)


def solution(mesh):
    fine = Mesh(mesh.devices.reshape(SIZES), AXES)
    spec = P(BLK, GRP)
    return jax.shard_map(body, mesh=fine, in_specs=(spec,) * 3, out_specs=spec, check_vma=False)
```

```python
import functools

import jax
import jax.numpy as jnp
from jax import lax
from jax.experimental import pallas as pl
from jax.experimental.pallas import tpu as pltpu
from jax.sharding import Mesh, PartitionSpec as P

prune_level = 0.5
TILE = 128
RB = 4
CB = 2
CAP = 4
META = 16
PACK = CAP * TILE + META
AXES = ("zh", "y", "x", "zl", "core")
SIZES = (2, 8, 4, 4, 2)
BLK = ("zh", "y")
GRP = ("x", "zl", "core")


SMEM = pl.BlockSpec(memory_space=pltpu.SMEM)
VMEM = pl.BlockSpec(memory_space=pltpu.VMEM)
BLOCK = (RB * TILE, CB * TILE)


def pack_kernel(pattern, matrix, *outs):
    count = jnp.int32(0)
    lane = lax.broadcasted_iota(jnp.int32, (META, TILE), 1)
    slots = jnp.full((META, TILE), CAP, jnp.int32)
    for t in range(RB * CB):
        r, s = divmod(t, CB)
        present = pattern[s, r] != 0
        slot = jnp.minimum(count, CAP - 1)

        @pl.when(present)
        def _():
            place = pl.multiple_of(slot * TILE, TILE)
            tile = matrix[r * TILE:(r + 1) * TILE, s * TILE:(s + 1) * TILE]
            for out in outs:
                for i in range(out.shape[0]):
                    out[i, pl.ds(place, TILE), :] = tile

        slots = jnp.where((lane == t) & present, slot, slots)
        count = count + present.astype(jnp.int32)
    head = slots.astype(jnp.float32).astype(jnp.bfloat16)
    for out in outs:
        for i in range(out.shape[0]):
            out[i, CAP * TILE:PACK, :] = head


def pack(matrix, pattern, copies):
    return pl.pallas_call(
        pack_kernel,
        out_shape=tuple(jax.ShapeDtypeStruct((n, PACK, TILE), jnp.bfloat16) for n in copies),
        in_specs=[SMEM, VMEM],
        out_specs=(VMEM,) * len(copies),
        name="pack_tiles",
    )(pattern.T, matrix)


def tile_of(ref, lead, table, row, t):
    slot = table[row, t]
    start = pl.multiple_of(jnp.minimum(slot, CAP - 1) * TILE, TILE)
    tile = ref[(*lead, pl.ds(start, TILE), slice(None))]
    return jnp.where(slot < CAP, tile, jnp.zeros_like(tile))


def read_slots(blocks, meta, table, sem):
    for i, (ref, lead) in enumerate(blocks):
        head = ref[(*lead, pl.ds(CAP * TILE, META), slice(None))]
        meta[i:i + 1, :] = head.astype(jnp.float32).astype(jnp.int32)[0:1]
    copy = pltpu.make_async_copy(meta, table, sem)
    copy.start()
    copy.wait()


def spread_band(band, table, chips, dense):
    nl = band.shape[1]
    for i, chip in enumerate(chips):
        for t in range(RB * CB):
            r, s = divmod(t, CB)
            k = (i * CB + s) * TILE
            dense[r * TILE:(r + 1) * TILE, k:k + TILE] = tile_of(band, (lax.div(chip, nl), lax.rem(chip, nl)), table, chip, t)


def spread_panel(panel, table, entry, core, owns):
    for z in range(2):
        for h, dense in enumerate(owns):
            owner = lax.rem(core + h, 2)
            for i in range(CB):
                for s in range(CB):
                    t = (owner * CB + i) * CB + s
                    at = (z * CB + i) * TILE
                    dense[at:at + TILE, s * TILE:(s + 1) * TILE] = tile_of(panel, (z,), table, entry + z, t)


def first_kernel(ny, place, mine, *rest):
    panels = dict(zip([j for j in range(ny) if j != ny // 2], rest[:ny - 1]))
    acc, spare, meta, table, a_dense, b_dense, sem = rest[ny - 1:]
    nx, nl = mine.shape[0], mine.shape[1]
    chips = nx * nl
    blocks = [(mine, (c // nl, c % nl)) for c in range(chips)]
    blocks += [(panel, (z,)) for panel in panels.values() for z in range(2)]
    read_slots(blocks, meta, table, sem)
    y, core = place[0], place[1]
    acc[...] = jnp.zeros_like(acc)
    for n, (j, panel) in enumerate(panels.items()):
        source = lax.rem(y - j + ny, ny)
        a, b = a_dense.at[n % 2], b_dense.at[n % 2]
        spread_panel(panel, table, chips + 2 * n, core, (b, spare.at[n]))
        spread_band(mine, table, (source, ny + source), a)
        acc[...] += jnp.dot(a[...], b[...], preferred_element_type=jnp.float32)


def second_kernel(ny, place, keep, mine, others, last, start, spare, out, totals, meta, table, a_dense, b_dense, acc, sem):
    nx, nl = mine.shape[0], mine.shape[1]
    chips = nx * nl
    y, core = place[0], place[1]
    source = lax.rem(y + ny // 2, ny)
    blocks = [(others, (c // nl, c % nl)) for c in range(chips)]
    blocks += [(last, (z,)) for z in range(2)]
    far = [source, ny + source]
    blocks += [(mine, (lax.div(chip, nl), lax.rem(chip, nl))) for chip in far]
    read_slots(blocks, meta, table, sem)
    own, other = b_dense.at[0], b_dense.at[1]
    spread_panel(last, table, chips, core, (own, other))
    for i, chip in enumerate(far):
        for t in range(RB * CB):
            r, s = divmod(t, CB)
            k = (i * CB + s) * TILE
            tile = tile_of(mine, (lax.div(chip, nl), lax.rem(chip, nl)), table, chips + 2 + i, t)
            a_dense[0, r * TILE:(r + 1) * TILE, k:k + TILE] = tile
    acc[...] = start[...] + jnp.dot(a_dense[0], own[...], preferred_element_type=jnp.float32)
    for n, j in enumerate([j for j in range(ny) if j != ny // 2] + [ny // 2]):
        source = lax.rem(y - j + ny, ny)
        a = a_dense.at[(n + 1) % 2]
        spread_band(others, table, (source, ny + source), a)
        b = spare[n] if n < ny - 1 else other[...]
        acc[...] += jnp.dot(a[...], b, preferred_element_type=jnp.float32)
    for s in range(CB):
        total = jnp.zeros((1, TILE), jnp.float32)
        for r in range(RB):
            at = (slice(r * TILE, (r + 1) * TILE), slice(s * TILE, (s + 1) * TILE))
            kept = acc[at] * keep[s, r].astype(jnp.float32)
            inflated = kept * kept
            out[at] = inflated
            total = total + jnp.sum(inflated, axis=0, keepdims=True)
        totals[:, s * TILE:(s + 1) * TILE] = total


def table_scratch(entries):
    return [pltpu.VMEM((entries, TILE), jnp.int32), pltpu.SMEM((entries, TILE), jnp.int32)]


HALF_COST = pl.CostEstimate(flops=2**30, bytes_accessed=2**23, transcendentals=0)
WIDE = (2, RB * TILE, 2 * CB * TILE)
DEEP = (2 * CB * TILE, CB * TILE)


def first_half(place, mine, panels):
    chips, ny = mine.shape[0] * mine.shape[1], len(panels) + 1
    return pl.pallas_call(
        functools.partial(first_kernel, ny),
        out_shape=(
            jax.ShapeDtypeStruct(BLOCK, jnp.float32),
            jax.ShapeDtypeStruct((ny - 1, *DEEP), jnp.bfloat16),
        ),
        in_specs=[SMEM] + [VMEM] * ny,
        out_specs=(VMEM, VMEM),
        scratch_shapes=table_scratch(chips + 2 * (ny - 1)) + [
            pltpu.VMEM(WIDE, jnp.bfloat16),
            pltpu.VMEM((2, *DEEP), jnp.bfloat16),
            pltpu.SemaphoreType.DMA,
        ],
        compiler_params=pltpu.CompilerParams(vmem_limit_bytes=24 * 2**20),
        cost_estimate=HALF_COST,
        name="first_half",
    )(place, mine, *panels)


def second_half(place, keep, mine, others, last, start, spare):
    chips, ny = mine.shape[0] * mine.shape[1], spare.shape[0] + 1
    return pl.pallas_call(
        functools.partial(second_kernel, ny),
        out_shape=(jax.ShapeDtypeStruct(BLOCK, jnp.float32), jax.ShapeDtypeStruct((1, CB * TILE), jnp.float32)),
        in_specs=[SMEM, SMEM] + [VMEM] * 5,
        out_specs=(VMEM, VMEM),
        scratch_shapes=table_scratch(chips + 4) + [
            pltpu.VMEM(WIDE, jnp.bfloat16),
            pltpu.VMEM((2, *DEEP), jnp.bfloat16),
            pltpu.VMEM(BLOCK, jnp.float32),
            pltpu.SemaphoreType.DMA,
        ],
        compiler_params=pltpu.CompilerParams(vmem_limit_bytes=24 * 2**20),
        cost_estimate=HALF_COST,
        name="second_half",
    )(place, keep.T, mine, others, last, start, spare)


def shifted(array, axis, by):
    n = lax.axis_size(axis)
    return lax.ppermute(array, axis, [(i, (i + by) % n) for i in range(n)])


def body(matrix, in_pattern, out_pattern):
    ny, nx, nl = lax.axis_size("y"), lax.axis_size("x"), lax.axis_size("zl")
    pair, copies = pack(matrix, in_pattern, (2, nl))
    own = lax.all_to_all(pair, "zh", 0, 0)
    line = lax.all_to_all(copies, "zl", 0, 0)
    up, down = [own], [own]
    for i in range(1, ny // 2):
        u, d = shifted(up[-1], "y", 1), shifted(down[-1], "y", -1)
        if i == 1:
            lines = jnp.broadcast_to(line, (nx, *line.shape))
            lines, u, d = lax.optimization_barrier((lines, u, d))
            mine = lax.all_to_all(lines, "x", 0, 0)
        elif i == ny // 2 - 1:
            mine, u, d = lax.optimization_barrier((mine, u, d))
        else:
            u, d = lax.optimization_barrier((u, d))
        up.append(u)
        down.append(d)
    last = shifted(up[-1], "y", 1)
    others = shifted(mine, "core", 1)
    place = jnp.stack([lax.axis_index(a) for a in ("y", "core")])
    start, spare = first_half(place, mine, [own] + up[1:] + down[:0:-1])
    inflated, totals = second_half(place, out_pattern, mine, others, last, start, spare)
    totals = totals + shifted(totals, "zh", 1)
    copies = jnp.broadcast_to(totals, (ny, totals.shape[1]))
    column_totals = jnp.sum(lax.all_to_all(copies, "y", 0, 0, tiled=True), axis=0, keepdims=True)
    scaled = inflated / column_totals * float(SIZES[0] * SIZES[1] * RB * TILE)
    return jnp.maximum(scaled - prune_level, 0.0).astype(jnp.bfloat16)


def solution(mesh):
    fine = Mesh(mesh.devices.reshape(SIZES), AXES)
    spec = P(BLK, GRP)
    return jax.shard_map(body, mesh=fine, in_specs=(spec,) * 3, out_specs=spec, check_vma=False)
```

```python
import functools

import jax
import jax.numpy as jnp
from jax import lax
from jax.experimental import pallas as pl
from jax.experimental.pallas import tpu as pltpu
from jax.sharding import Mesh, PartitionSpec as P

prune_level = 0.5
TILE = 128
RB = 4
CB = 2
CAP = 4
HEAD = 16
SIGNS = 4
LEAST = 2.0**-126
PACK = CAP * TILE
AXES = ("zh", "y", "x", "zl", "core")
SIZES = (2, 8, 4, 4, 2)
BLK = ("zh", "y")
GRP = ("x", "zl", "core")


SMEM = pl.BlockSpec(memory_space=pltpu.SMEM)
VMEM = pl.BlockSpec(memory_space=pltpu.VMEM)
BLOCK = (RB * TILE, CB * TILE)


def pack_kernel(pattern, matrix, out):
    lane = lax.broadcasted_iota(jnp.int32, (HEAD, TILE), 1)
    row = lax.broadcasted_iota(jnp.int32, (HEAD, TILE), 0)
    signs = (row == 0) & (lane < SIGNS)
    for slot in range(CAP):
        out[0, slot * TILE:slot * TILE + HEAD, :] = jnp.ones((HEAD, TILE), jnp.bfloat16)
    count = jnp.int32(0)
    for t in range(RB * CB):
        r, s = divmod(t, CB)
        present = pattern[s, r] != 0
        slot = jnp.minimum(count, CAP - 1)

        @pl.when(present)
        def _():
            place = pl.multiple_of(slot * TILE, TILE)
            tile = matrix[r * TILE:(r + 1) * TILE, s * TILE:(s + 1) * TILE]
            head = tile[:HEAD].astype(jnp.float32)
            size = jnp.maximum(head, LEAST)
            bit = lax.shift_right_logical(jnp.full_like(lane, t + RB * CB), jnp.minimum(lane, SIGNS)) & 1
            head = jnp.where(signs, jnp.where(bit == 1, -size, size), head)
            out[0, pl.ds(place, HEAD), :] = head.astype(jnp.bfloat16)
            out[0, pl.ds(pl.multiple_of(place + HEAD, HEAD), TILE - HEAD), :] = tile[HEAD:]

        count = count + present.astype(jnp.int32)


def pack(matrix, pattern):
    return pl.pallas_call(
        pack_kernel,
        out_shape=jax.ShapeDtypeStruct((1, PACK, TILE), jnp.bfloat16),
        in_specs=[SMEM, VMEM],
        out_specs=VMEM,
        name="pack_tiles",
    )(pattern.T, matrix)


def put_tile(dense, at, ref, lead, table, row, t):
    slot = table[row, t]
    start = pl.multiple_of(jnp.minimum(slot, CAP - 1) * TILE, TILE)
    head = jnp.abs(ref[(*lead, pl.ds(start, HEAD), slice(None))])
    rest = ref[(*lead, pl.ds(pl.multiple_of(start + HEAD, HEAD), TILE - HEAD), slice(None))]
    r, c = at
    dense[r:r + HEAD, c:c + TILE] = jnp.where(slot < CAP, head, jnp.zeros_like(head))
    dense[r + HEAD:r + TILE, c:c + TILE] = jnp.where(slot < CAP, rest, jnp.zeros_like(rest))


def read_slots(blocks, heads, meta, table, sem):
    for i, (ref, lead) in enumerate(blocks):
        for slot in range(CAP):
            head = ref[(*lead, pl.ds(slot * TILE, HEAD), slice(None))].astype(jnp.float32)
            heads[slot, i:i + 1, :] = head[0:1]
    lane = lax.broadcasted_iota(jnp.int32, meta.shape, 1)
    weight = jnp.where(lane < SIGNS, lax.shift_left(jnp.ones_like(lane), jnp.minimum(lane, SIGNS)), 0)
    slots = jnp.full(meta.shape, CAP, jnp.int32)
    for slot in range(CAP):
        code = jnp.sum(jnp.where(heads[slot] < 0, weight, 0), axis=1, keepdims=True)
        slots = jnp.where(code == lane + RB * CB, slot, slots)
    meta[...] = slots
    copy = pltpu.make_async_copy(meta, table, sem)
    copy.start()
    copy.wait()


def spread_band(band, table, entries, places, dense, col):
    for i, (entry, lead) in enumerate(zip(entries, places)):
        for t in range(RB * CB):
            r, s = divmod(t, CB)
            k = col + (i * CB + s) * TILE
            put_tile(dense, (r * TILE, k), band, lead, table, entry, t)


def spread_panel(panel, table, entry, core, owns):
    for z in range(2):
        for h, (dense, row) in enumerate(owns):
            owner = lax.rem(core + h, 2)
            for i in range(CB):
                for s in range(CB):
                    t = (owner * CB + i) * CB + s
                    at = row + (z * CB + i) * TILE
                    put_tile(dense, (at, s * TILE), panel, (z,), table, entry + z, t)


def sources(hi, y, ny, nl, js):
    for j in js:
        source = lax.rem(y - j + ny, ny)
        chips = (hi * ny + source, (1 - hi) * ny + source)
        yield chips, [(lax.div(chip, nl), lax.rem(chip, nl)) for chip in chips]


def all_blocks(band):
    return [(band, (x, k)) for x in range(band.shape[0]) for k in range(band.shape[1])]


def own_kernel(ny, js, far, place, mine, *rest):
    panels, rest = rest[:len(js)], rest[len(js):]
    start, rest = (rest[0], rest[1:]) if far else (None, rest)
    acc, spare, rest = rest[0], rest[1], rest[2:]
    far_dense, rest = (rest[0], rest[1:]) if far else (None, rest)
    heads, meta, table, a_dense, b_dense, sem = rest
    hi, y, core = place[0], place[1], place[2]
    nl = mine.shape[1]
    blocks = all_blocks(mine)
    chips = len(blocks)
    blocks += [(panel, (z,)) for panel in panels for z in range(2)]
    read_slots(blocks, heads, meta, table, sem)
    for n, (entries, places) in enumerate(sources(hi, y, ny, nl, js)):
        spread_panel(panels[n], table, chips + 2 * n, core, ((b_dense, n * DEEP), (spare, n * DEEP)))
        spread_band(mine, table, entries, places, a_dense, n * DEEP)
    total = jnp.dot(a_dense[...], b_dense[...], preferred_element_type=jnp.float32)
    acc[...] = total if start is None else start[...] + total
    if far:
        ((entries, places),) = sources(hi, y, ny, nl, [ny // 2])
        spread_band(mine, table, entries, places, far_dense, 0)


def other_kernel(ny, order, place, others, start, *rest):
    spares, (acc, far_dense, heads, meta, table, a_dense, sem) = rest[:len(order)], rest[len(order):]
    hi, y = place[0], place[1]
    nl = others.shape[1]
    read_slots(all_blocks(others), heads, meta, table, sem)
    total = start[...]
    col = 0
    for js, spare in zip(order, spares):
        depth = len(js) * DEEP
        for n, (entries, places) in enumerate(sources(hi, y, ny, nl, js)):
            spread_band(others, table, entries, places, a_dense, col + n * DEEP)
        total += jnp.dot(a_dense[:, col:col + depth], spare[...], preferred_element_type=jnp.float32)
        col += depth
    acc[...] = total
    ((entries, places),) = sources(hi, y, ny, nl, [ny // 2])
    spread_band(others, table, entries, places, far_dense, 0)


def last_kernel(place, keep, last, start, far_mine, far_others, out, totals, heads, meta, table, b_dense, acc, sem):
    core = place[2]
    read_slots([(last, (z,)) for z in range(2)], heads, meta, table, sem)
    mine_rows, others_rows = b_dense.at[pl.ds(0, DEEP)], b_dense.at[pl.ds(DEEP, DEEP)]
    spread_panel(last, table, 0, core, ((mine_rows, 0), (others_rows, 0)))
    total = start[...] + jnp.dot(far_mine[...], mine_rows[...], preferred_element_type=jnp.float32)
    acc[...] = total + jnp.dot(far_others[...], others_rows[...], preferred_element_type=jnp.float32)
    for s in range(CB):
        total = jnp.zeros((1, TILE), jnp.float32)
        for r in range(RB):
            at = (slice(r * TILE, (r + 1) * TILE), slice(s * TILE, (s + 1) * TILE))
            kept = acc[at] * keep[s, r].astype(jnp.float32)
            inflated = kept * kept
            out[at] = inflated
            total = total + jnp.sum(inflated, axis=0, keepdims=True)
        totals[:, s * TILE:(s + 1) * TILE] = total


def scratch(entries, *more):
    return [
        pltpu.VMEM((CAP, entries, TILE), jnp.float32),
        pltpu.VMEM((entries, TILE), jnp.int32),
        pltpu.SMEM((entries, TILE), jnp.int32),
        *more,
        pltpu.SemaphoreType.DMA,
    ]


def kernel_call(kernel, name, outs, smems, vmems, scratch_shapes):
    return pl.pallas_call(
        kernel,
        out_shape=outs,
        in_specs=[SMEM] * len(smems) + [VMEM] * len(vmems),
        out_specs=jax.tree.map(lambda _: VMEM, outs),
        scratch_shapes=scratch_shapes,
        compiler_params=pltpu.CompilerParams(vmem_limit_bytes=24 * 2**20),
        cost_estimate=pl.CostEstimate(flops=2**35, bytes_accessed=2**23, transcendentals=0),
        name=name,
    )(*smems, *vmems)


DEEP = 2 * CB * TILE
BLOCK_SUM = jax.ShapeDtypeStruct(BLOCK, jnp.float32)
FAR = jax.ShapeDtypeStruct((RB * TILE, DEEP), jnp.bfloat16)


def rows_of(count):
    return (count * DEEP, CB * TILE)


def own_part(ny, js, place, mine, panels, start=None):
    chips = mine.shape[0] * mine.shape[1]
    far = start is not None
    outs = (BLOCK_SUM, jax.ShapeDtypeStruct(rows_of(len(js)), jnp.bfloat16)) + ((FAR,) if far else ())
    shapes = scratch(
        chips + 2 * len(js),
        pltpu.VMEM((RB * TILE, len(js) * DEEP), jnp.bfloat16),
        pltpu.VMEM(rows_of(len(js)), jnp.bfloat16),
    )
    arrays = [mine, *panels] + ([start] if far else [])
    return kernel_call(functools.partial(own_kernel, ny, js, far), "own_part", outs, [place], arrays, shapes)


def other_part(ny, order, place, others, start, spares):
    chips = others.shape[0] * others.shape[1]
    shapes = scratch(chips, pltpu.VMEM((RB * TILE, sum(map(len, order)) * DEEP), jnp.bfloat16))
    arrays = [others, start, *spares]
    return kernel_call(functools.partial(other_kernel, ny, order), "other_part", (BLOCK_SUM, FAR), [place], arrays, shapes)


def last_part(place, keep, last, start, far_mine, far_others):
    outs = (BLOCK_SUM, jax.ShapeDtypeStruct((1, CB * TILE), jnp.float32))
    shapes = scratch(2, pltpu.VMEM(rows_of(2), jnp.bfloat16), pltpu.VMEM(BLOCK, jnp.float32))
    arrays = [last, start, far_mine, far_others]
    return kernel_call(last_kernel, "last_part", outs, [place, keep.T], arrays, shapes)


def shifted(array, axis, by):
    n = lax.axis_size(axis)
    return lax.ppermute(array, axis, [(i, (i + by) % n) for i in range(n)])


def body(matrix, in_pattern, out_pattern):
    ny, nx, nl = lax.axis_size("y"), lax.axis_size("x"), lax.axis_size("zl")
    packed = pack(matrix, in_pattern)
    other = shifted(packed, "zh", 1)
    line = lax.all_gather(packed, "zl", tiled=True)
    line, other = lax.optimization_barrier((line, other))
    own = jnp.concatenate([packed, other])
    mine = lax.all_to_all(jnp.broadcast_to(line, (nx, *line.shape)), "x", 0, 0)
    place = jnp.stack([lax.axis_index(a) for a in ("zh", "y", "core")])
    half = ny // 2
    panels = {0: own}
    for i in range(1, half):
        panels[i] = shifted(panels[i - 1], "y", 1)
        panels[ny - i] = shifted(panels[(ny - i + 1) % ny], "y", -1)
    early = [j for j in range(ny) if min(j, ny - j) < half - 1]
    late = [half - 1, half + 1]
    start, spare = own_part(ny, early, place, mine, [panels[j] for j in early])
    sent, _, _ = lax.optimization_barrier((mine, panels[half - 2], panels[half + 2]))
    others = shifted(sent, "core", 1)
    last = shifted(panels[half - 1], "y", 1)
    start, late_spare, far_mine = own_part(ny, late, place, mine, [panels[j] for j in late], start)
    start, far_others = other_part(ny, [early, late], place, others, start, [spare, late_spare])
    inflated, totals = last_part(place, out_pattern, last, start, far_mine, far_others)
    totals = totals + shifted(totals, "zh", 1)
    copies = jnp.broadcast_to(totals, (ny, totals.shape[1]))
    column_totals = jnp.sum(lax.all_to_all(copies, "y", 0, 0, tiled=True), axis=0, keepdims=True)
    scaled = inflated / column_totals * float(SIZES[0] * SIZES[1] * RB * TILE)
    return jnp.maximum(scaled - prune_level, 0.0).astype(jnp.bfloat16)


def solution(mesh):
    fine = Mesh(mesh.devices.reshape(SIZES), AXES)
    spec = P(BLK, GRP)
    return jax.shard_map(body, mesh=fine, in_specs=(spec,) * 3, out_specs=spec, check_vma=False)
```

```python
import functools

import jax
import jax.numpy as jnp
from jax import lax
from jax.experimental import pallas as pl
from jax.experimental.pallas import tpu as pltpu
from jax.sharding import Mesh, PartitionSpec as P

prune_level = 0.5
TILE = 128
RB = 4
CB = 2
CAP = 4
HEAD = 16
SIGNS = 4
SLOT_BITS = 3
LEAST = 2.0**-126
PACK = CAP * TILE
AXES = ("zh", "y", "x", "zl", "core")
SIZES = (2, 8, 4, 4, 2)
BLK = ("zh", "y")
GRP = ("x", "zl", "core")


SMEM = pl.BlockSpec(memory_space=pltpu.SMEM)
VMEM = pl.BlockSpec(memory_space=pltpu.VMEM)
BLOCK = (RB * TILE, CB * TILE)


def pack_kernel(pattern, matrix, out):
    lane = lax.broadcasted_iota(jnp.int32, (HEAD, TILE), 1)
    row = lax.broadcasted_iota(jnp.int32, (HEAD, TILE), 0)
    signs = (row == 0) & (lane < SIGNS)
    for slot in range(CAP):
        out[0, slot * TILE:slot * TILE + HEAD, :] = jnp.ones((HEAD, TILE), jnp.bfloat16)
    count = jnp.int32(0)
    for t in range(RB * CB):
        r, s = divmod(t, CB)
        present = pattern[s, r] != 0
        slot = jnp.minimum(count, CAP - 1)

        @pl.when(present)
        def _():
            place = pl.multiple_of(slot * TILE, TILE)
            tile = matrix[r * TILE:(r + 1) * TILE, s * TILE:(s + 1) * TILE]
            head = tile[:HEAD].astype(jnp.float32)
            size = jnp.maximum(head, LEAST)
            bit = lax.shift_right_logical(jnp.full_like(lane, t + RB * CB), jnp.minimum(lane, SIGNS)) & 1
            head = jnp.where(signs, jnp.where(bit == 1, -size, size), head)
            out[0, pl.ds(place, HEAD), :] = head.astype(jnp.bfloat16)
            out[0, pl.ds(pl.multiple_of(place + HEAD, HEAD), TILE - HEAD), :] = tile[HEAD:]

        count = count + present.astype(jnp.int32)


def pack(matrix, pattern):
    return pl.pallas_call(
        pack_kernel,
        out_shape=jax.ShapeDtypeStruct((1, PACK, TILE), jnp.bfloat16),
        in_specs=[SMEM, VMEM],
        out_specs=VMEM,
        name="pack_tiles",
    )(pattern.T, matrix)


def put_tile(dense, at, ref, lead, table, row, t):
    slot = lax.shift_right_logical(table[row], SLOT_BITS * t) & (2**SLOT_BITS - 1)
    start = pl.multiple_of(jnp.minimum(slot, CAP - 1) * TILE, TILE)
    head = jnp.abs(ref[(*lead, pl.ds(start, HEAD), slice(None))])
    rest = ref[(*lead, pl.ds(pl.multiple_of(start + HEAD, HEAD), TILE - HEAD), slice(None))]
    r, c = at
    dense[r:r + HEAD, c:c + TILE] = jnp.where(slot < CAP, head, jnp.zeros_like(head))
    dense[r + HEAD:r + TILE, c:c + TILE] = jnp.where(slot < CAP, rest, jnp.zeros_like(rest))


def read_slots(blocks, heads, table):
    for i, (ref, lead) in enumerate(blocks):
        for slot in range(CAP):
            head = ref[(*lead, pl.ds(slot * TILE, HEAD), slice(None))].astype(jnp.float32)
            heads[slot, i:i + 1, :] = head[0:1]
    lane = lax.broadcasted_iota(jnp.int32, heads.shape[1:], 1)
    weight = jnp.where(lane < SIGNS, lax.shift_left(jnp.ones_like(lane), jnp.minimum(lane, SIGNS)), 0)
    slots = jnp.full(lane.shape, CAP, jnp.int32)
    for slot in range(CAP):
        code = jnp.sum(jnp.where(heads[slot] < 0, weight, 0), axis=1, keepdims=True)
        slots = jnp.where(code == lane + RB * CB, slot, slots)
    tiles = RB * CB
    slots = jnp.where(lane < tiles, lax.shift_left(slots, SLOT_BITS * jnp.minimum(lane, tiles - 1)), 0)
    slots = jnp.sum(slots, axis=1, keepdims=True)
    for i in range(len(blocks)):
        table[i] = slots[i, 0]


def spread_band(band, table, entries, places, dense, col):
    for i, (entry, lead) in enumerate(zip(entries, places)):
        for t in range(RB * CB):
            r, s = divmod(t, CB)
            k = col + (i * CB + s) * TILE
            put_tile(dense, (r * TILE, k), band, lead, table, entry, t)


def spread_panel(panel, table, entry, core, owns):
    for z in range(2):
        for h, (dense, row) in enumerate(owns):
            owner = lax.rem(core + h, 2)
            for i in range(CB):
                for s in range(CB):
                    t = (owner * CB + i) * CB + s
                    at = row + (z * CB + i) * TILE
                    put_tile(dense, (at, s * TILE), panel, (z,), table, entry + z, t)


def sources(hi, y, ny, nl, js):
    for j in js:
        source = lax.rem(y - j + ny, ny)
        chips = (hi * ny + source, (1 - hi) * ny + source)
        yield chips, [(lax.div(chip, nl), lax.rem(chip, nl)) for chip in chips]


def all_blocks(band):
    return [(band, (x, k)) for x in range(band.shape[0]) for k in range(band.shape[1])]


def own_kernel(ny, js, far, place, mine, *rest):
    panels, rest = rest[:len(js)], rest[len(js):]
    start, rest = (rest[0], rest[1:]) if far else (None, rest)
    acc, spare, rest = rest[0], rest[1], rest[2:]
    far_dense, rest = (rest[0], rest[1:]) if far else (None, rest)
    heads, table, a_dense, b_dense = rest
    hi, y, core = place[0], place[1], place[2]
    nl = mine.shape[1]
    blocks = all_blocks(mine)
    chips = len(blocks)
    blocks += [(panel, (z,)) for panel in panels for z in range(2)]
    read_slots(blocks, heads, table)
    for n, (entries, places) in enumerate(sources(hi, y, ny, nl, js)):
        spread_panel(panels[n], table, chips + 2 * n, core, ((b_dense, n * DEEP), (spare, n * DEEP)))
        spread_band(mine, table, entries, places, a_dense, n * DEEP)
    total = jnp.dot(a_dense[...], b_dense[...], preferred_element_type=jnp.float32)
    acc[...] = total if start is None else start[...] + total
    if far:
        ((entries, places),) = sources(hi, y, ny, nl, [ny // 2])
        spread_band(mine, table, entries, places, far_dense, 0)


def other_kernel(ny, order, place, others, start, *rest):
    spares, (acc, far_dense, heads, table, a_dense) = rest[:len(order)], rest[len(order):]
    hi, y = place[0], place[1]
    nl = others.shape[1]
    read_slots(all_blocks(others), heads, table)
    total = start[...]
    col = 0
    for js, spare in zip(order, spares):
        depth = len(js) * DEEP
        for n, (entries, places) in enumerate(sources(hi, y, ny, nl, js)):
            spread_band(others, table, entries, places, a_dense, col + n * DEEP)
        total += jnp.dot(a_dense[:, col:col + depth], spare[...], preferred_element_type=jnp.float32)
        col += depth
    acc[...] = total
    ((entries, places),) = sources(hi, y, ny, nl, [ny // 2])
    spread_band(others, table, entries, places, far_dense, 0)


def last_kernel(place, keep, last, start, far_mine, far_others, out, totals, heads, table, b_dense, acc):
    core = place[2]
    read_slots([(last, (z,)) for z in range(2)], heads, table)
    mine_rows, others_rows = b_dense.at[pl.ds(0, DEEP)], b_dense.at[pl.ds(DEEP, DEEP)]
    spread_panel(last, table, 0, core, ((mine_rows, 0), (others_rows, 0)))
    total = start[...] + jnp.dot(far_mine[...], mine_rows[...], preferred_element_type=jnp.float32)
    acc[...] = total + jnp.dot(far_others[...], others_rows[...], preferred_element_type=jnp.float32)
    for s in range(CB):
        total = jnp.zeros((1, TILE), jnp.float32)
        for r in range(RB):
            at = (slice(r * TILE, (r + 1) * TILE), slice(s * TILE, (s + 1) * TILE))
            kept = acc[at] * keep[s, r].astype(jnp.float32)
            inflated = kept * kept
            out[at] = inflated
            total = total + jnp.sum(inflated, axis=0, keepdims=True)
        totals[:, s * TILE:(s + 1) * TILE] = total


def scratch(entries, *more):
    return [
        pltpu.VMEM((CAP, entries, TILE), jnp.float32),
        pltpu.SMEM((entries,), jnp.int32),
        *more,
    ]


def kernel_call(kernel, name, outs, smems, vmems, scratch_shapes):
    return pl.pallas_call(
        kernel,
        out_shape=outs,
        in_specs=[SMEM] * len(smems) + [VMEM] * len(vmems),
        out_specs=jax.tree.map(lambda _: VMEM, outs),
        scratch_shapes=scratch_shapes,
        compiler_params=pltpu.CompilerParams(vmem_limit_bytes=24 * 2**20),
        cost_estimate=pl.CostEstimate(flops=2**35, bytes_accessed=2**23, transcendentals=0),
        name=name,
    )(*smems, *vmems)


DEEP = 2 * CB * TILE
BLOCK_SUM = jax.ShapeDtypeStruct(BLOCK, jnp.float32)
FAR = jax.ShapeDtypeStruct((RB * TILE, DEEP), jnp.bfloat16)


def rows_of(count):
    return (count * DEEP, CB * TILE)


def own_part(ny, js, place, mine, panels, start=None):
    chips = mine.shape[0] * mine.shape[1]
    far = start is not None
    outs = (BLOCK_SUM, jax.ShapeDtypeStruct(rows_of(len(js)), jnp.bfloat16)) + ((FAR,) if far else ())
    shapes = scratch(
        chips + 2 * len(js),
        pltpu.VMEM((RB * TILE, len(js) * DEEP), jnp.bfloat16),
        pltpu.VMEM(rows_of(len(js)), jnp.bfloat16),
    )
    arrays = [mine, *panels] + ([start] if far else [])
    return kernel_call(functools.partial(own_kernel, ny, js, far), "own_part", outs, [place], arrays, shapes)


def other_part(ny, order, place, others, start, spares):
    chips = others.shape[0] * others.shape[1]
    shapes = scratch(chips, pltpu.VMEM((RB * TILE, sum(map(len, order)) * DEEP), jnp.bfloat16))
    arrays = [others, start, *spares]
    return kernel_call(functools.partial(other_kernel, ny, order), "other_part", (BLOCK_SUM, FAR), [place], arrays, shapes)


def last_part(place, keep, last, start, far_mine, far_others):
    outs = (BLOCK_SUM, jax.ShapeDtypeStruct((1, CB * TILE), jnp.float32))
    shapes = scratch(2, pltpu.VMEM(rows_of(2), jnp.bfloat16), pltpu.VMEM(BLOCK, jnp.float32))
    arrays = [last, start, far_mine, far_others]
    return kernel_call(last_kernel, "last_part", outs, [place, keep.T], arrays, shapes)


def shifted(array, axis, by):
    n = lax.axis_size(axis)
    return lax.ppermute(array, axis, [(i, (i + by) % n) for i in range(n)])


def body(matrix, in_pattern, out_pattern):
    ny, nx, nl = lax.axis_size("y"), lax.axis_size("x"), lax.axis_size("zl")
    packed = pack(matrix, in_pattern)
    other = shifted(packed, "zh", 1)
    line = lax.all_gather(packed, "zl", tiled=True)
    line, other = lax.optimization_barrier((line, other))
    own = jnp.concatenate([packed, other])
    mine = lax.all_to_all(jnp.broadcast_to(line, (nx, *line.shape)), "x", 0, 0)
    place = jnp.stack([lax.axis_index(a) for a in ("zh", "y", "core")])
    half = ny // 2
    panels = {0: own}
    for i in range(1, half):
        panels[i] = shifted(panels[i - 1], "y", 1)
        panels[ny - i] = shifted(panels[(ny - i + 1) % ny], "y", -1)
    early = [j for j in range(ny) if min(j, ny - j) < half - 1]
    late = [half - 1, half + 1]
    start, spare = own_part(ny, early, place, mine, [panels[j] for j in early])
    sent, start, panels[half - 1] = lax.optimization_barrier((mine, start, panels[half - 1]))
    others = shifted(sent, "core", 1)
    last = shifted(panels[half - 1], "y", 1)
    start, late_spare, far_mine = own_part(ny, late, place, mine, [panels[j] for j in late], start)
    start, far_others = other_part(ny, [early, late], place, others, start, [spare, late_spare])
    inflated, totals = last_part(place, out_pattern, last, start, far_mine, far_others)
    copies = jnp.broadcast_to(totals, (ny * lax.axis_size("zh"), totals.shape[1]))
    column_totals = jnp.sum(lax.all_to_all(copies, BLK, 0, 0, tiled=True), axis=0, keepdims=True)
    scaled = inflated / column_totals * float(SIZES[0] * SIZES[1] * RB * TILE)
    return jnp.maximum(scaled - prune_level, 0.0).astype(jnp.bfloat16)


def solution(mesh):
    fine = Mesh(mesh.devices.reshape(SIZES), AXES)
    spec = P(BLK, GRP)
    return jax.shard_map(body, mesh=fine, in_specs=(spec,) * 3, out_specs=spec, check_vma=False)
```

```python
import functools

import jax
import jax.numpy as jnp
from jax import lax
from jax.experimental import pallas as pl
from jax.experimental.pallas import tpu as pltpu
from jax.sharding import Mesh, PartitionSpec as P

prune_level = 0.5
TILE = 128
RB = 4
CB = 2
CAP = 4
HEAD = 16
SIGNS = 4
SLOT_BITS = 3
LEAST = 2.0**-126
PACK = CAP * TILE
AXES = ("zh", "y", "x", "zl", "core")
SIZES = (2, 8, 4, 4, 2)
BLK = ("zh", "y")
GRP = ("x", "zl", "core")


SMEM = pl.BlockSpec(memory_space=pltpu.SMEM)
VMEM = pl.BlockSpec(memory_space=pltpu.VMEM)
BLOCK = (RB * TILE, CB * TILE)


def pack_kernel(pattern, matrix, out):
    lane = lax.broadcasted_iota(jnp.int32, (HEAD, TILE), 1)
    row = lax.broadcasted_iota(jnp.int32, (HEAD, TILE), 0)
    signs = (row == 0) & (lane < SIGNS)
    for slot in range(CAP):
        out[0, slot * TILE:slot * TILE + HEAD, :] = jnp.ones((HEAD, TILE), jnp.bfloat16)
    count = jnp.int32(0)
    for t in range(RB * CB):
        r, s = divmod(t, CB)
        present = pattern[s, r] != 0
        slot = jnp.minimum(count, CAP - 1)

        @pl.when(present)
        def _():
            place = pl.multiple_of(slot * TILE, TILE)
            tile = matrix[r * TILE:(r + 1) * TILE, s * TILE:(s + 1) * TILE]
            head = tile[:HEAD].astype(jnp.float32)
            size = jnp.maximum(head, LEAST)
            bit = lax.shift_right_logical(jnp.full_like(lane, t + RB * CB), jnp.minimum(lane, SIGNS)) & 1
            head = jnp.where(signs, jnp.where(bit == 1, -size, size), head)
            out[0, pl.ds(place, HEAD), :] = head.astype(jnp.bfloat16)
            out[0, pl.ds(pl.multiple_of(place + HEAD, HEAD), TILE - HEAD), :] = tile[HEAD:]

        count = count + present.astype(jnp.int32)


def pack(matrix, pattern):
    return pl.pallas_call(
        pack_kernel,
        out_shape=jax.ShapeDtypeStruct((1, PACK, TILE), jnp.bfloat16),
        in_specs=[SMEM, VMEM],
        out_specs=VMEM,
        name="pack_tiles",
    )(pattern.T, matrix)


def put_tile(dense, at, ref, lead, table, row, t):
    slot = lax.shift_right_logical(table[row], SLOT_BITS * t) & (2**SLOT_BITS - 1)
    start = pl.multiple_of(jnp.minimum(slot, CAP - 1) * TILE, TILE)
    head = jnp.abs(ref[(*lead, pl.ds(start, HEAD), slice(None))])
    rest = ref[(*lead, pl.ds(pl.multiple_of(start + HEAD, HEAD), TILE - HEAD), slice(None))]
    r, c = at
    dense[r:r + HEAD, c:c + TILE] = jnp.where(slot < CAP, head, jnp.zeros_like(head))
    dense[r + HEAD:r + TILE, c:c + TILE] = jnp.where(slot < CAP, rest, jnp.zeros_like(rest))


def read_slots(blocks, heads, table):
    for i, (ref, lead) in enumerate(blocks):
        for slot in range(CAP):
            head = ref[(*lead, pl.ds(slot * TILE, HEAD), slice(None))].astype(jnp.float32)
            heads[slot, i:i + 1, :] = head[0:1]
    lane = lax.broadcasted_iota(jnp.int32, heads.shape[1:], 1)
    weight = jnp.where(lane < SIGNS, lax.shift_left(jnp.ones_like(lane), jnp.minimum(lane, SIGNS)), 0)
    slots = jnp.full(lane.shape, CAP, jnp.int32)
    for slot in range(CAP):
        code = jnp.sum(jnp.where(heads[slot] < 0, weight, 0), axis=1, keepdims=True)
        slots = jnp.where(code == lane + RB * CB, slot, slots)
    tiles = RB * CB
    slots = jnp.where(lane < tiles, lax.shift_left(slots, SLOT_BITS * jnp.minimum(lane, tiles - 1)), 0)
    slots = jnp.sum(slots, axis=1, keepdims=True)
    for i in range(len(blocks)):
        table[i] = slots[i, 0]


def spread_band(band, table, entries, places, dense, col):
    for i, (entry, lead) in enumerate(zip(entries, places)):
        for t in range(RB * CB):
            r, s = divmod(t, CB)
            k = col + (i * CB + s) * TILE
            put_tile(dense, (r * TILE, k), band, lead, table, entry, t)


def spread_panel(panel, table, entry, core, owns):
    for z in range(2):
        for h, (dense, row) in enumerate(owns):
            owner = lax.rem(core + h, 2)
            for i in range(CB):
                for s in range(CB):
                    t = (owner * CB + i) * CB + s
                    at = row + (z * CB + i) * TILE
                    put_tile(dense, (at, s * TILE), panel, (z,), table, entry + z, t)


def sources(hi, y, ny, nl, js):
    for j in js:
        source = lax.rem(y - j + ny, ny)
        chips = (hi * ny + source, (1 - hi) * ny + source)
        yield chips, [(lax.div(chip, nl), lax.rem(chip, nl)) for chip in chips]


def all_blocks(band):
    return [(band, (x, k)) for x in range(band.shape[0]) for k in range(band.shape[1])]


def own_kernel(ny, js, more, far, place, mine, *rest):
    panels, rest = rest[:len(js)], rest[len(js):]
    start, rest = (rest[0], rest[1:]) if more else (None, rest)
    acc, spare, rest = rest[0], rest[1], rest[2:]
    far_dense, rest = (rest[0], rest[1:]) if far else (None, rest)
    heads, table, a_dense, b_dense = rest
    hi, y, core = place[0], place[1], place[2]
    nl = mine.shape[1]
    blocks = all_blocks(mine)
    chips = len(blocks)
    blocks += [(panel, (z,)) for panel in panels for z in range(2)]
    read_slots(blocks, heads, table)
    for n, (entries, places) in enumerate(sources(hi, y, ny, nl, js)):
        spread_panel(panels[n], table, chips + 2 * n, core, ((b_dense, n * DEEP), (spare, n * DEEP)))
        spread_band(mine, table, entries, places, a_dense, n * DEEP)
    total = jnp.dot(a_dense[...], b_dense[...], preferred_element_type=jnp.float32)
    acc[...] = total if start is None else start[...] + total
    if far:
        ((entries, places),) = sources(hi, y, ny, nl, [ny // 2])
        spread_band(mine, table, entries, places, far_dense, 0)


def other_kernel(ny, order, place, others, start, *rest):
    spares, (acc, far_dense, heads, table, a_dense) = rest[:len(order)], rest[len(order):]
    hi, y = place[0], place[1]
    nl = others.shape[1]
    read_slots(all_blocks(others), heads, table)
    total = start[...]
    col = 0
    for js, spare in zip(order, spares):
        depth = len(js) * DEEP
        for n, (entries, places) in enumerate(sources(hi, y, ny, nl, js)):
            spread_band(others, table, entries, places, a_dense, col + n * DEEP)
        total += jnp.dot(a_dense[:, col:col + depth], spare[...], preferred_element_type=jnp.float32)
        col += depth
    acc[...] = total
    ((entries, places),) = sources(hi, y, ny, nl, [ny // 2])
    spread_band(others, table, entries, places, far_dense, 0)


def last_kernel(place, keep, last, start, far_mine, far_others, out, totals, heads, table, b_dense, acc):
    core = place[2]
    read_slots([(last, (z,)) for z in range(2)], heads, table)
    mine_rows, others_rows = b_dense.at[pl.ds(0, DEEP)], b_dense.at[pl.ds(DEEP, DEEP)]
    spread_panel(last, table, 0, core, ((mine_rows, 0), (others_rows, 0)))
    total = start[...] + jnp.dot(far_mine[...], mine_rows[...], preferred_element_type=jnp.float32)
    acc[...] = total + jnp.dot(far_others[...], others_rows[...], preferred_element_type=jnp.float32)
    for s in range(CB):
        total = jnp.zeros((1, TILE), jnp.float32)
        for r in range(RB):
            at = (slice(r * TILE, (r + 1) * TILE), slice(s * TILE, (s + 1) * TILE))
            kept = acc[at] * keep[s, r].astype(jnp.float32)
            inflated = kept * kept
            out[at] = inflated
            total = total + jnp.sum(inflated, axis=0, keepdims=True)
        totals[:, s * TILE:(s + 1) * TILE] = total


def scratch(entries, *more):
    return [
        pltpu.VMEM((CAP, entries, TILE), jnp.float32),
        pltpu.SMEM((entries,), jnp.int32),
        *more,
    ]


def kernel_call(kernel, name, outs, smems, vmems, scratch_shapes, flops=2**30):
    return pl.pallas_call(
        kernel,
        out_shape=outs,
        in_specs=[SMEM] * len(smems) + [VMEM] * len(vmems),
        out_specs=jax.tree.map(lambda _: VMEM, outs),
        scratch_shapes=scratch_shapes,
        compiler_params=pltpu.CompilerParams(vmem_limit_bytes=24 * 2**20),
        cost_estimate=pl.CostEstimate(flops=flops, bytes_accessed=2**23, transcendentals=0),
        name=name,
    )(*smems, *vmems)


DEEP = 2 * CB * TILE
BLOCK_SUM = jax.ShapeDtypeStruct(BLOCK, jnp.float32)
FAR = jax.ShapeDtypeStruct((RB * TILE, DEEP), jnp.bfloat16)


def rows_of(count):
    return (count * DEEP, CB * TILE)


def own_part(ny, js, place, mine, panels, start=None, far=False):
    chips = mine.shape[0] * mine.shape[1]
    more = start is not None
    outs = (BLOCK_SUM, jax.ShapeDtypeStruct(rows_of(len(js)), jnp.bfloat16)) + ((FAR,) if far else ())
    shapes = scratch(
        chips + 2 * len(js),
        pltpu.VMEM((RB * TILE, len(js) * DEEP), jnp.bfloat16),
        pltpu.VMEM(rows_of(len(js)), jnp.bfloat16),
    )
    arrays = [mine, *panels] + ([start] if more else [])
    return kernel_call(functools.partial(own_kernel, ny, js, more, far), "own_part", outs, [place], arrays, shapes, 2**30 if far else 2**35)


def other_part(ny, order, place, others, start, spares):
    chips = others.shape[0] * others.shape[1]
    shapes = scratch(chips, pltpu.VMEM((RB * TILE, sum(map(len, order)) * DEEP), jnp.bfloat16))
    arrays = [others, start, *spares]
    return kernel_call(functools.partial(other_kernel, ny, order), "other_part", (BLOCK_SUM, FAR), [place], arrays, shapes)


def last_part(place, keep, last, start, far_mine, far_others):
    outs = (BLOCK_SUM, jax.ShapeDtypeStruct((1, CB * TILE), jnp.float32))
    shapes = scratch(2, pltpu.VMEM(rows_of(2), jnp.bfloat16), pltpu.VMEM(BLOCK, jnp.float32))
    arrays = [last, start, far_mine, far_others]
    return kernel_call(last_kernel, "last_part", outs, [place, keep.T], arrays, shapes)


def shifted(array, axis, by):
    n = lax.axis_size(axis)
    return lax.ppermute(array, axis, [(i, (i + by) % n) for i in range(n)])


def body(matrix, in_pattern, out_pattern):
    ny, nx, nl = lax.axis_size("y"), lax.axis_size("x"), lax.axis_size("zl")
    packed = pack(matrix, in_pattern)
    other = shifted(packed, "zh", 1)
    line = lax.all_gather(packed, "zl", tiled=True)
    line, other = lax.optimization_barrier((line, other))
    own = jnp.concatenate([packed, other])
    mine = lax.all_to_all(jnp.broadcast_to(line, (nx, *line.shape)), "x", 0, 0)
    place = jnp.stack([lax.axis_index(a) for a in ("zh", "y", "core")])
    half = ny // 2
    panels = {0: own}
    for i in range(1, half):
        panels[i] = shifted(panels[i - 1], "y", 1)
        panels[ny - i] = shifted(panels[(ny - i + 1) % ny], "y", -1)
    first = [j for j in range(ny) if min(j, ny - j) < half - 2]
    second = [half - 2, half + 2]
    late = [half - 1, half + 1]
    start, spare = own_part(ny, first, place, mine, [panels[j] for j in first])
    sent, start, panels[half + 1] = lax.optimization_barrier((mine, start, panels[half + 1]))
    others = shifted(sent, "core", 1)
    start, second_spare = own_part(ny, second, place, mine, [panels[j] for j in second], start)
    last = shifted(panels[half + 1], "y", -1)
    start, late_spare, far_mine = own_part(ny, late, place, mine, [panels[j] for j in late], start, True)
    start, far_others = other_part(ny, [first, second, late], place, others, start, [spare, second_spare, late_spare])
    inflated, totals = last_part(place, out_pattern, last, start, far_mine, far_others)
    copies = jnp.broadcast_to(totals, (ny * lax.axis_size("zh"), totals.shape[1]))
    column_totals = jnp.sum(lax.all_to_all(copies, BLK, 0, 0, tiled=True), axis=0, keepdims=True)
    scaled = inflated / column_totals * float(SIZES[0] * SIZES[1] * RB * TILE)
    return jnp.maximum(scaled - prune_level, 0.0).astype(jnp.bfloat16)


def solution(mesh):
    fine = Mesh(mesh.devices.reshape(SIZES), AXES)
    spec = P(BLK, GRP)
    return jax.shard_map(body, mesh=fine, in_specs=(spec,) * 3, out_specs=spec, check_vma=False)
```

```python
import functools

import jax
import jax.numpy as jnp
from jax import lax
from jax.experimental import pallas as pl
from jax.experimental.pallas import tpu as pltpu
from jax.sharding import Mesh, PartitionSpec as P

prune_level = 0.5
TILE = 128
RB = 4
CB = 2
CAP = 4
HEAD = 16
SIGNS = 4
SLOT_BITS = 3
LEAST = 2.0**-126
PACK = CAP * TILE
AXES = ("zh", "y", "x", "zl", "core")
SIZES = (2, 8, 4, 4, 2)
BLK = ("zh", "y")
GRP = ("x", "zl", "core")


SMEM = pl.BlockSpec(memory_space=pltpu.SMEM)
VMEM = pl.BlockSpec(memory_space=pltpu.VMEM)
BLOCK = (RB * TILE, CB * TILE)


def pack_kernel(pattern, matrix, out):
    lane = lax.broadcasted_iota(jnp.int32, (HEAD, TILE), 1)
    row = lax.broadcasted_iota(jnp.int32, (HEAD, TILE), 0)
    signs = (row == 0) & (lane < SIGNS)
    for slot in range(CAP):
        out[0, slot * TILE:slot * TILE + HEAD, :] = jnp.ones((HEAD, TILE), jnp.bfloat16)
    count = jnp.int32(0)
    for t in range(RB * CB):
        r, s = divmod(t, CB)
        present = pattern[s, r] != 0
        slot = jnp.minimum(count, CAP - 1)

        @pl.when(present)
        def _():
            place = pl.multiple_of(slot * TILE, TILE)
            tile = matrix[r * TILE:(r + 1) * TILE, s * TILE:(s + 1) * TILE]
            head = tile[:HEAD].astype(jnp.float32)
            size = jnp.maximum(head, LEAST)
            bit = lax.shift_right_logical(jnp.full_like(lane, t + RB * CB), jnp.minimum(lane, SIGNS)) & 1
            head = jnp.where(signs, jnp.where(bit == 1, -size, size), head)
            out[0, pl.ds(place, HEAD), :] = head.astype(jnp.bfloat16)
            out[0, pl.ds(pl.multiple_of(place + HEAD, HEAD), TILE - HEAD), :] = tile[HEAD:]

        count = count + present.astype(jnp.int32)


def pack(matrix, pattern):
    return pl.pallas_call(
        pack_kernel,
        out_shape=jax.ShapeDtypeStruct((1, PACK, TILE), jnp.bfloat16),
        in_specs=[SMEM, VMEM],
        out_specs=VMEM,
        name="pack_tiles",
    )(pattern.T, matrix)


def put_tile(dense, at, ref, lead, table, row, t):
    slot = lax.shift_right_logical(table[row], SLOT_BITS * t) & (2**SLOT_BITS - 1)
    start = pl.multiple_of(jnp.minimum(slot, CAP - 1) * TILE, TILE)
    head = jnp.abs(ref[(*lead, pl.ds(start, HEAD), slice(None))])
    rest = ref[(*lead, pl.ds(pl.multiple_of(start + HEAD, HEAD), TILE - HEAD), slice(None))]
    r, c = at
    dense[r:r + HEAD, c:c + TILE] = jnp.where(slot < CAP, head, jnp.zeros_like(head))
    dense[r + HEAD:r + TILE, c:c + TILE] = jnp.where(slot < CAP, rest, jnp.zeros_like(rest))


def read_slots(blocks, heads, table):
    for i, (ref, lead) in enumerate(blocks):
        for slot in range(CAP):
            head = ref[(*lead, pl.ds(slot * TILE, HEAD), slice(None))].astype(jnp.float32)
            heads[slot, i:i + 1, :] = head[0:1]
    lane = lax.broadcasted_iota(jnp.int32, heads.shape[1:], 1)
    weight = jnp.where(lane < SIGNS, lax.shift_left(jnp.ones_like(lane), jnp.minimum(lane, SIGNS)), 0)
    slots = jnp.full(lane.shape, CAP, jnp.int32)
    for slot in range(CAP):
        code = jnp.sum(jnp.where(heads[slot] < 0, weight, 0), axis=1, keepdims=True)
        slots = jnp.where(code == lane + RB * CB, slot, slots)
    tiles = RB * CB
    slots = jnp.where(lane < tiles, lax.shift_left(slots, SLOT_BITS * jnp.minimum(lane, tiles - 1)), 0)
    slots = jnp.sum(slots, axis=1, keepdims=True)
    for i in range(len(blocks)):
        table[i] = slots[i, 0]


def spread_band(band, table, entries, places, dense, col):
    for i, (entry, lead) in enumerate(zip(entries, places)):
        for t in range(RB * CB):
            r, s = divmod(t, CB)
            k = col + (i * CB + s) * TILE
            put_tile(dense, (r * TILE, k), band, lead, table, entry, t)


def spread_panel(panel, table, entry, core, owns):
    for z in range(2):
        for h, (dense, row) in enumerate(owns):
            owner = lax.rem(core + h, 2)
            for i in range(CB):
                for s in range(CB):
                    t = (owner * CB + i) * CB + s
                    at = row + (z * CB + i) * TILE
                    put_tile(dense, (at, s * TILE), panel, (z,), table, entry + z, t)


def sources(hi, y, ny, nl, js):
    for j in js:
        source = lax.rem(y - j + ny, ny)
        chips = (hi * ny + source, (1 - hi) * ny + source)
        yield chips, [(lax.div(chip, nl), lax.rem(chip, nl)) for chip in chips]


def all_blocks(band):
    return [(band, (x, k)) for x in range(band.shape[0]) for k in range(band.shape[1])]


def own_kernel(ny, js, more, far, place, mine, *rest):
    panels, rest = rest[:len(js)], rest[len(js):]
    start, rest = (rest[0], rest[1:]) if more else (None, rest)
    acc, spare, rest = rest[0], rest[1], rest[2:]
    far_dense, rest = (rest[0], rest[1:]) if far else (None, rest)
    heads, table, a_dense, b_dense = rest
    hi, y, core = place[0], place[1], place[2]
    nl = mine.shape[1]
    blocks = all_blocks(mine)
    chips = len(blocks)
    blocks += [(panel, (z,)) for panel in panels for z in range(2)]
    read_slots(blocks, heads, table)
    for n, (entries, places) in enumerate(sources(hi, y, ny, nl, js)):
        spread_panel(panels[n], table, chips + 2 * n, core, ((b_dense, n * DEEP), (spare, n * DEEP)))
        spread_band(mine, table, entries, places, a_dense, n * DEEP)
    total = jnp.dot(a_dense[...], b_dense[...], preferred_element_type=jnp.float32)
    acc[...] = total if start is None else start[...] + total
    if far:
        ((entries, places),) = sources(hi, y, ny, nl, [ny // 2])
        spread_band(mine, table, entries, places, far_dense, 0)


def final_kernel(ny, order, place, keep, others, last, start, far_mine, *rest):
    spares, (out, totals, heads, table, last_heads, last_table, a_dense, b_dense, acc) = rest[:len(order)], rest[len(order):]
    hi, y, core = place[0], place[1], place[2]
    nl = others.shape[1]
    read_slots(all_blocks(others), heads, table)
    read_slots([(last, (z,)) for z in range(2)], last_heads, last_table)
    total = start[...]
    col = 0
    for js, spare in zip(order, spares):
        depth = len(js) * DEEP
        for n, (entries, places) in enumerate(sources(hi, y, ny, nl, js)):
            spread_band(others, table, entries, places, a_dense, col + n * DEEP)
        total += jnp.dot(a_dense[:, col:col + depth], spare[...], preferred_element_type=jnp.float32)
        col += depth
    ((entries, places),) = sources(hi, y, ny, nl, [ny // 2])
    spread_band(others, table, entries, places, a_dense, col)
    mine_rows, others_rows = b_dense.at[pl.ds(0, DEEP)], b_dense.at[pl.ds(DEEP, DEEP)]
    spread_panel(last, last_table, 0, core, ((mine_rows, 0), (others_rows, 0)))
    total += jnp.dot(far_mine[...], mine_rows[...], preferred_element_type=jnp.float32)
    acc[...] = total + jnp.dot(a_dense[:, col:col + DEEP], others_rows[...], preferred_element_type=jnp.float32)
    for s in range(CB):
        total = jnp.zeros((1, TILE), jnp.float32)
        for r in range(RB):
            at = (slice(r * TILE, (r + 1) * TILE), slice(s * TILE, (s + 1) * TILE))
            kept = acc[at] * keep[s, r].astype(jnp.float32)
            inflated = kept * kept
            out[at] = inflated
            total = total + jnp.sum(inflated, axis=0, keepdims=True)
        totals[:, s * TILE:(s + 1) * TILE] = total


def copies_kernel(line, out, sems):
    copies = [pltpu.make_async_copy(line, out.at[i], sems.at[i]) for i in range(out.shape[0])]
    for copy in copies:
        copy.start()
    for copy in copies:
        copy.wait()


def copies_of(line, count):
    return pl.pallas_call(
        copies_kernel,
        out_shape=jax.ShapeDtypeStruct((count, *line.shape), line.dtype),
        in_specs=[VMEM],
        out_specs=pl.BlockSpec(memory_space=pl.ANY),
        scratch_shapes=[pltpu.SemaphoreType.DMA((count,))],
        compiler_params=pltpu.CompilerParams(vmem_limit_bytes=8 * 2**20),
        name="line_copies",
    )(line)


def scratch(entries, *more):
    return [
        pltpu.VMEM((CAP, entries, TILE), jnp.float32),
        pltpu.SMEM((entries,), jnp.int32),
        *more,
    ]


def kernel_call(kernel, name, outs, smems, vmems, scratch_shapes, flops=2**30):
    return pl.pallas_call(
        kernel,
        out_shape=outs,
        in_specs=[SMEM] * len(smems) + [VMEM] * len(vmems),
        out_specs=jax.tree.map(lambda _: VMEM, outs),
        scratch_shapes=scratch_shapes,
        compiler_params=pltpu.CompilerParams(vmem_limit_bytes=24 * 2**20),
        cost_estimate=pl.CostEstimate(flops=flops, bytes_accessed=2**23, transcendentals=0),
        name=name,
    )(*smems, *vmems)


DEEP = 2 * CB * TILE
BLOCK_SUM = jax.ShapeDtypeStruct(BLOCK, jnp.float32)
FAR = jax.ShapeDtypeStruct((RB * TILE, DEEP), jnp.bfloat16)


def rows_of(count):
    return (count * DEEP, CB * TILE)


def own_part(ny, js, place, mine, panels, start=None, far=False):
    chips = mine.shape[0] * mine.shape[1]
    more = start is not None
    outs = (BLOCK_SUM, jax.ShapeDtypeStruct(rows_of(len(js)), jnp.bfloat16)) + ((FAR,) if far else ())
    shapes = scratch(
        chips + 2 * len(js),
        pltpu.VMEM((RB * TILE, len(js) * DEEP), jnp.bfloat16),
        pltpu.VMEM(rows_of(len(js)), jnp.bfloat16),
    )
    arrays = [mine, *panels] + ([start] if more else [])
    return kernel_call(functools.partial(own_kernel, ny, js, more, far), "own_part", outs, [place], arrays, shapes, 2**35)


def final_part(ny, order, place, keep, others, last, start, far_mine, spares):
    chips = others.shape[0] * others.shape[1]
    outs = (BLOCK_SUM, jax.ShapeDtypeStruct((1, CB * TILE), jnp.float32))
    shapes = scratch(chips) + scratch(
        2,
        pltpu.VMEM((RB * TILE, ny * DEEP), jnp.bfloat16),
        pltpu.VMEM(rows_of(2), jnp.bfloat16),
        pltpu.VMEM(BLOCK, jnp.float32),
    )
    arrays = [others, last, start, far_mine, *spares]
    return kernel_call(functools.partial(final_kernel, ny, order), "final_part", outs, [place, keep.T], arrays, shapes)


def shifted(array, axis, by):
    n = lax.axis_size(axis)
    return lax.ppermute(array, axis, [(i, (i + by) % n) for i in range(n)])


def body(matrix, in_pattern, out_pattern):
    ny, nx, nl = lax.axis_size("y"), lax.axis_size("x"), lax.axis_size("zl")
    packed = pack(matrix, in_pattern)
    other = shifted(packed, "zh", 1)
    line = lax.all_gather(packed, "zl", tiled=True)
    line, other = lax.optimization_barrier((line, other))
    own = jnp.concatenate([packed, other])
    mine = lax.all_to_all(copies_of(line, nx), "x", 0, 0)
    place = jnp.stack([lax.axis_index(a) for a in ("zh", "y", "core")])
    half = ny // 2
    panels = {0: own}
    for i in range(1, half):
        panels[i] = shifted(panels[i - 1], "y", 1)
        panels[ny - i] = shifted(panels[(ny - i + 1) % ny], "y", -1)
    first = [j for j in range(ny) if min(j, ny - j) < half - 2]
    late = [half - 2, half + 2, half - 1, half + 1]
    start, spare = own_part(ny, first, place, mine, [panels[j] for j in first])
    sent, start, panels[half + 1] = lax.optimization_barrier((mine, start, panels[half + 1]))
    others = shifted(sent, "core", 1)
    last = shifted(panels[half + 1], "y", -1)
    start, late_spare, far_mine = own_part(ny, late, place, mine, [panels[j] for j in late], start, True)
    inflated, totals = final_part(ny, [first, late], place, out_pattern, others, last, start, far_mine, [spare, late_spare])
    copies = jnp.broadcast_to(totals, (ny * lax.axis_size("zh"), totals.shape[1]))
    column_totals = jnp.sum(lax.all_to_all(copies, BLK, 0, 0, tiled=True), axis=0, keepdims=True)
    scaled = inflated / column_totals * float(SIZES[0] * SIZES[1] * RB * TILE)
    return jnp.maximum(scaled - prune_level, 0.0).astype(jnp.bfloat16)


def solution(mesh):
    fine = Mesh(mesh.devices.reshape(SIZES), AXES)
    spec = P(BLK, GRP)
    return jax.shard_map(body, mesh=fine, in_specs=(spec,) * 3, out_specs=spec, check_vma=False)
```

```python
import functools

import jax
import jax.numpy as jnp
from jax import lax
from jax.experimental import pallas as pl
from jax.experimental.pallas import tpu as pltpu
from jax.sharding import Mesh, PartitionSpec as P

prune_level = 0.5
TILE = 128
RB = 4
CB = 2
CAP = 4
HEAD = 16
SIGNS = 4
SLOT_BITS = 3
LEAST = 2.0**-126
PACK = CAP * TILE
AXES = ("zh", "y", "x", "zl", "core")
SIZES = (2, 8, 4, 4, 2)
BLK = ("zh", "y")
GRP = ("x", "zl", "core")


SMEM = pl.BlockSpec(memory_space=pltpu.SMEM)
VMEM = pl.BlockSpec(memory_space=pltpu.VMEM)
BLOCK = (RB * TILE, CB * TILE)


def pack_kernel(pattern, matrix, out):
    lane = lax.broadcasted_iota(jnp.int32, (HEAD, TILE), 1)
    row = lax.broadcasted_iota(jnp.int32, (HEAD, TILE), 0)
    signs = (row == 0) & (lane < SIGNS)
    for slot in range(CAP):
        out[0, slot * TILE:slot * TILE + HEAD, :] = jnp.ones((HEAD, TILE), jnp.bfloat16)
    count = jnp.int32(0)
    for t in range(RB * CB):
        r, s = divmod(t, CB)
        present = pattern[s, r] != 0
        slot = jnp.minimum(count, CAP - 1)

        @pl.when(present)
        def _():
            place = pl.multiple_of(slot * TILE, TILE)
            tile = matrix[r * TILE:(r + 1) * TILE, s * TILE:(s + 1) * TILE]
            head = tile[:HEAD].astype(jnp.float32)
            size = jnp.maximum(head, LEAST)
            bit = lax.shift_right_logical(jnp.full_like(lane, t + RB * CB), jnp.minimum(lane, SIGNS)) & 1
            head = jnp.where(signs, jnp.where(bit == 1, -size, size), head)
            out[0, pl.ds(place, HEAD), :] = head.astype(jnp.bfloat16)
            out[0, pl.ds(pl.multiple_of(place + HEAD, HEAD), TILE - HEAD), :] = tile[HEAD:]

        count = count + present.astype(jnp.int32)


def pack(matrix, pattern):
    return pl.pallas_call(
        pack_kernel,
        out_shape=jax.ShapeDtypeStruct((1, PACK, TILE), jnp.bfloat16),
        in_specs=[SMEM, VMEM],
        out_specs=VMEM,
        name="pack_tiles",
    )(pattern.T, matrix)


def slot_of(table, row, t):
    return lax.shift_right_logical(table[row], SLOT_BITS * t) & (2**SLOT_BITS - 1)


def put_tile(dense, at, ref, lead, table, row, t):
    slot = slot_of(table, row, t)
    start = pl.multiple_of(jnp.minimum(slot, CAP - 1) * TILE, TILE)
    head = jnp.abs(ref[(*lead, pl.ds(start, HEAD), slice(None))])
    rest = ref[(*lead, pl.ds(pl.multiple_of(start + HEAD, HEAD), TILE - HEAD), slice(None))]
    r, c = at
    dense[r:r + HEAD, c:c + TILE] = jnp.where(slot < CAP, head, jnp.zeros_like(head))
    dense[r + HEAD:r + TILE, c:c + TILE] = jnp.where(slot < CAP, rest, jnp.zeros_like(rest))


def read_slots(blocks, heads, table):
    for i, (ref, lead) in enumerate(blocks):
        for slot in range(CAP):
            head = ref[(*lead, pl.ds(slot * TILE, HEAD), slice(None))].astype(jnp.float32)
            heads[slot, i:i + 1, :] = head[0:1]
    lane = lax.broadcasted_iota(jnp.int32, heads.shape[1:], 1)
    weight = jnp.where(lane < SIGNS, lax.shift_left(jnp.ones_like(lane), jnp.minimum(lane, SIGNS)), 0)
    slots = jnp.full(lane.shape, CAP, jnp.int32)
    for slot in range(CAP):
        code = jnp.sum(jnp.where(heads[slot] < 0, weight, 0), axis=1, keepdims=True)
        slots = jnp.where(code == lane + RB * CB, slot, slots)
    tiles = RB * CB
    slots = jnp.where(lane < tiles, lax.shift_left(slots, SLOT_BITS * jnp.minimum(lane, tiles - 1)), 0)
    slots = jnp.sum(slots, axis=1, keepdims=True)
    for i in range(len(blocks)):
        table[i] = slots[i, 0]


def band_columns(band, table, entries, places):
    rows = []
    for r in range(RB):
        tiles = []
        for entry, lead in zip(entries, places):
            for s in range(CB):
                slot = slot_of(table, entry, r * CB + s)
                start = pl.multiple_of(jnp.minimum(slot, CAP - 1) * TILE, TILE)
                tile = jnp.abs(band[(*lead, pl.ds(start, TILE), slice(None))])
                tiles.append(jnp.where(slot < CAP, tile, jnp.zeros_like(tile)))
        rows.append(jnp.concatenate(tiles, axis=1))
    return jnp.concatenate(rows, axis=0)


def spread_panel(panel, table, entry, core, owns):
    for z in range(2):
        for h, (dense, row) in enumerate(owns):
            owner = lax.rem(core + h, 2)
            for i in range(CB):
                for s in range(CB):
                    t = (owner * CB + i) * CB + s
                    at = row + (z * CB + i) * TILE
                    put_tile(dense, (at, s * TILE), panel, (z,), table, entry + z, t)


def sources(hi, y, ny, nl, js):
    for j in js:
        source = lax.rem(y - j + ny, ny)
        chips = (hi * ny + source, (1 - hi) * ny + source)
        yield chips, [(lax.div(chip, nl), lax.rem(chip, nl)) for chip in chips]


def all_blocks(band):
    return [(band, (x, k)) for x in range(band.shape[0]) for k in range(band.shape[1])]


def own_kernel(ny, js, place, mine, *rest):
    panels, (acc, spare, far_dense, heads, table, b_dense) = rest[:len(js)], rest[len(js):]
    hi, y, core = place[0], place[1], place[2]
    nl = mine.shape[1]
    blocks = all_blocks(mine)
    chips = len(blocks)
    blocks += [(panel, (z,)) for panel in panels for z in range(2)]
    read_slots(blocks, heads, table)
    for n, (entries, places) in enumerate(sources(hi, y, ny, nl, js)):
        spread_panel(panels[n], table, chips + 2 * n, core, ((b_dense, n * DEEP), (spare, n * DEEP)))
        columns = band_columns(mine, table, entries, places)
        part = jnp.dot(columns, b_dense[n * DEEP:(n + 1) * DEEP], preferred_element_type=jnp.float32)
        acc[...] = part if n == 0 else acc[...] + part
    ((entries, places),) = sources(hi, y, ny, nl, [ny // 2])
    far_dense[...] = band_columns(mine, table, entries, places)


def final_kernel(
    ny, js, place, keep, others, last, start, far_mine, spare, out, totals,
    heads, table, last_heads, last_table, b_dense, acc,
):
    hi, y, core = place[0], place[1], place[2]
    nl = others.shape[1]
    read_slots(all_blocks(others), heads, table)
    read_slots([(last, (z,)) for z in range(2)], last_heads, last_table)
    acc[...] = start[...]
    for n, (entries, places) in enumerate(sources(hi, y, ny, nl, js)):
        columns = band_columns(others, table, entries, places)
        acc[...] += jnp.dot(columns, spare[n * DEEP:(n + 1) * DEEP], preferred_element_type=jnp.float32)
    mine_rows, others_rows = b_dense.at[pl.ds(0, DEEP)], b_dense.at[pl.ds(DEEP, DEEP)]
    spread_panel(last, last_table, 0, core, ((mine_rows, 0), (others_rows, 0)))
    acc[...] += jnp.dot(far_mine[...], mine_rows[...], preferred_element_type=jnp.float32)
    ((entries, places),) = sources(hi, y, ny, nl, [ny // 2])
    columns = band_columns(others, table, entries, places)
    acc[...] += jnp.dot(columns, others_rows[...], preferred_element_type=jnp.float32)
    for s in range(CB):
        total = jnp.zeros((1, TILE), jnp.float32)
        for r in range(RB):
            at = (slice(r * TILE, (r + 1) * TILE), slice(s * TILE, (s + 1) * TILE))
            kept = acc[at] * keep[s, r].astype(jnp.float32)
            inflated = kept * kept
            out[at] = inflated
            total = total + jnp.sum(inflated, axis=0, keepdims=True)
        totals[:, s * TILE:(s + 1) * TILE] = total


def copies_kernel(line, out, sems):
    copies = [pltpu.make_async_copy(line, out.at[i], sems.at[i]) for i in range(out.shape[0])]
    for copy in copies:
        copy.start()
    for copy in copies:
        copy.wait()


def copies_of(line, count):
    return pl.pallas_call(
        copies_kernel,
        out_shape=jax.ShapeDtypeStruct((count, *line.shape), line.dtype),
        in_specs=[VMEM],
        out_specs=pl.BlockSpec(memory_space=pl.ANY),
        scratch_shapes=[pltpu.SemaphoreType.DMA((count,))],
        compiler_params=pltpu.CompilerParams(vmem_limit_bytes=8 * 2**20),
        name="line_copies",
    )(line)


def scratch(entries, *more):
    return [
        pltpu.VMEM((CAP, entries, TILE), jnp.float32),
        pltpu.SMEM((entries,), jnp.int32),
        *more,
    ]


def kernel_call(kernel, name, outs, smems, vmems, scratch_shapes):
    return pl.pallas_call(
        kernel,
        out_shape=outs,
        in_specs=[SMEM] * len(smems) + [VMEM] * len(vmems),
        out_specs=jax.tree.map(lambda _: VMEM, outs),
        scratch_shapes=scratch_shapes,
        compiler_params=pltpu.CompilerParams(vmem_limit_bytes=24 * 2**20),
        cost_estimate=pl.CostEstimate(flops=2**35, bytes_accessed=2**23, transcendentals=0),
        name=name,
    )(*smems, *vmems)


DEEP = 2 * CB * TILE
BLOCK_SUM = jax.ShapeDtypeStruct(BLOCK, jnp.float32)
FAR = jax.ShapeDtypeStruct((RB * TILE, DEEP), jnp.bfloat16)


def rows_of(count):
    return (count * DEEP, CB * TILE)


def own_part(ny, js, place, mine, panels):
    chips = mine.shape[0] * mine.shape[1]
    outs = (BLOCK_SUM, jax.ShapeDtypeStruct(rows_of(len(js)), jnp.bfloat16), FAR)
    shapes = scratch(
        chips + 2 * len(js),
        pltpu.VMEM(rows_of(len(js)), jnp.bfloat16),
    )
    return kernel_call(functools.partial(own_kernel, ny, js), "own_part", outs, [place], [mine, *panels], shapes)


def final_part(ny, js, place, keep, others, last, start, far_mine, spare):
    chips = others.shape[0] * others.shape[1]
    outs = (BLOCK_SUM, jax.ShapeDtypeStruct((1, CB * TILE), jnp.float32))
    shapes = scratch(chips) + scratch(
        2,
        pltpu.VMEM(rows_of(2), jnp.bfloat16),
        pltpu.VMEM(BLOCK, jnp.float32),
    )
    arrays = [others, last, start, far_mine, spare]
    return kernel_call(functools.partial(final_kernel, ny, js), "final_part", outs, [place, keep.T], arrays, shapes)


def again_kernel(block, out):
    out[...] = block[...]


def again(block):
    return pl.pallas_call(
        again_kernel,
        out_shape=jax.ShapeDtypeStruct(block.shape, block.dtype),
        in_specs=[VMEM],
        out_specs=VMEM,
        compiler_params=pltpu.CompilerParams(vmem_limit_bytes=4 * 2**20),
        cost_estimate=pl.CostEstimate(flops=2**36, bytes_accessed=2**20, transcendentals=0),
        name="both_again",
    )(block)


def shifted(array, axis, by):
    n = lax.axis_size(axis)
    return lax.ppermute(array, axis, [(i, (i + by) % n) for i in range(n)])


def body(matrix, in_pattern, out_pattern):
    ny, nx, nl = lax.axis_size("y"), lax.axis_size("x"), lax.axis_size("zl")
    packed = pack(matrix, in_pattern)
    other = shifted(packed, "zh", 1)
    line = lax.all_gather(packed, "zl", tiled=True)
    line, other = lax.optimization_barrier((line, other))
    own = jnp.concatenate([packed, other])
    mine = lax.all_to_all(copies_of(line, nx), "x", 0, 0)
    place = jnp.stack([lax.axis_index(a) for a in ("zh", "y", "core")])
    half = ny // 2
    panels = {0: own}
    for i in range(1, half):
        panels[i] = shifted(again(own) if i == 1 else panels[i - 1], "y", 1)
        panels[ny - i] = shifted(panels[(ny - i + 1) % ny], "y", -1)
    near = [j for j in range(ny) if j != half]
    sent, panels[half + 1] = lax.optimization_barrier((mine, panels[half + 1]))
    others = shifted(sent, "core", 1)
    last = shifted(panels[half + 1], "y", -1)
    start, spare, far_mine = own_part(ny, near, place, mine, [panels[j] for j in near])
    inflated, totals = final_part(ny, near, place, out_pattern, others, last, start, far_mine, spare)
    copies = jnp.broadcast_to(totals, (ny * lax.axis_size("zh"), totals.shape[1]))
    column_totals = jnp.sum(lax.all_to_all(copies, BLK, 0, 0, tiled=True), axis=0, keepdims=True)
    scaled = inflated / column_totals * float(SIZES[0] * SIZES[1] * RB * TILE)
    return jnp.maximum(scaled - prune_level, 0.0).astype(jnp.bfloat16)


def solution(mesh):
    fine = Mesh(mesh.devices.reshape(SIZES), AXES)
    spec = P(BLK, GRP)
    return jax.shard_map(body, mesh=fine, in_specs=(spec,) * 3, out_specs=spec, check_vma=False)
```

```python
import functools

import jax
import jax.numpy as jnp
from jax import lax
from jax.experimental import pallas as pl
from jax.experimental.pallas import tpu as pltpu
from jax.sharding import Mesh, PartitionSpec as P

prune_level = 0.5
TILE = 128
RB = 4
CB = 2
CAP = 4
HEAD = 16
SIGNS = 4
SLOT_BITS = 3
LEAST = 2.0**-126
PACK = CAP * TILE
AXES = ("zh", "y", "x", "zl", "core")
SIZES = (2, 8, 4, 4, 2)
BLK = ("zh", "y")
GRP = ("x", "zl", "core")


SMEM = pl.BlockSpec(memory_space=pltpu.SMEM)
VMEM = pl.BlockSpec(memory_space=pltpu.VMEM)
BLOCK = (RB * TILE, CB * TILE)


def pack_kernel(pattern_in, matrix_in, out, pattern, matrix, sems):
    pattern_copy = pltpu.make_async_copy(pattern_in, pattern, sems.at[0])
    matrix_copy = pltpu.make_async_copy(matrix_in, matrix, sems.at[1])
    matrix_copy.start()
    pattern_copy.start()
    lane = lax.broadcasted_iota(jnp.int32, (HEAD, TILE), 1)
    row = lax.broadcasted_iota(jnp.int32, (HEAD, TILE), 0)
    signs = (row == 0) & (lane < SIGNS)
    for slot in range(CAP):
        out[0, slot * TILE:slot * TILE + HEAD, :] = jnp.ones((HEAD, TILE), jnp.bfloat16)
    pattern_copy.wait()
    matrix_copy.wait()
    count = jnp.int32(0)
    for t in range(RB * CB):
        r, s = divmod(t, CB)
        present = pattern[s, r] != 0
        slot = jnp.minimum(count, CAP - 1)

        @pl.when(present)
        def _():
            place = pl.multiple_of(slot * TILE, TILE)
            tile = matrix[r * TILE:(r + 1) * TILE, s * TILE:(s + 1) * TILE]
            head = tile[:HEAD].astype(jnp.float32)
            size = jnp.maximum(head, LEAST)
            bit = lax.shift_right_logical(jnp.full_like(lane, t + RB * CB), jnp.minimum(lane, SIGNS)) & 1
            head = jnp.where(signs, jnp.where(bit == 1, -size, size), head)
            out[0, pl.ds(place, HEAD), :] = head.astype(jnp.bfloat16)
            out[0, pl.ds(pl.multiple_of(place + HEAD, HEAD), TILE - HEAD), :] = tile[HEAD:]

        count = count + present.astype(jnp.int32)


def pack(matrix, pattern):
    return pl.pallas_call(
        pack_kernel,
        out_shape=jax.ShapeDtypeStruct((1, PACK, TILE), jnp.bfloat16),
        in_specs=[pl.BlockSpec(memory_space=pl.ANY)] * 2,
        out_specs=VMEM,
        scratch_shapes=[
            pltpu.SMEM((CB, RB), jnp.int32),
            pltpu.VMEM(BLOCK, jnp.bfloat16),
            pltpu.SemaphoreType.DMA((2,)),
        ],
        name="pack_tiles",
    )(pattern.T, matrix)


def slot_of(table, row, t):
    return lax.shift_right_logical(table[row], SLOT_BITS * t) & (2**SLOT_BITS - 1)


def put_tile(dense, at, ref, lead, table, row, t):
    slot = slot_of(table, row, t)
    start = pl.multiple_of(jnp.minimum(slot, CAP - 1) * TILE, TILE)
    head = jnp.abs(ref[(*lead, pl.ds(start, HEAD), slice(None))])
    rest = ref[(*lead, pl.ds(pl.multiple_of(start + HEAD, HEAD), TILE - HEAD), slice(None))]
    r, c = at
    dense[r:r + HEAD, c:c + TILE] = jnp.where(slot < CAP, head, jnp.zeros_like(head))
    dense[r + HEAD:r + TILE, c:c + TILE] = jnp.where(slot < CAP, rest, jnp.zeros_like(rest))


def read_slots(blocks, heads, table):
    for i, (ref, lead) in enumerate(blocks):
        for slot in range(CAP):
            head = ref[(*lead, pl.ds(slot * TILE, HEAD), slice(None))].astype(jnp.float32)
            heads[slot, i:i + 1, :] = head[0:1]
    lane = lax.broadcasted_iota(jnp.int32, heads.shape[1:], 1)
    weight = jnp.where(lane < SIGNS, lax.shift_left(jnp.ones_like(lane), jnp.minimum(lane, SIGNS)), 0)
    slots = jnp.full(lane.shape, CAP, jnp.int32)
    for slot in range(CAP):
        code = jnp.sum(jnp.where(heads[slot] < 0, weight, 0), axis=1, keepdims=True)
        slots = jnp.where(code == lane + RB * CB, slot, slots)
    tiles = RB * CB
    slots = jnp.where(lane < tiles, lax.shift_left(slots, SLOT_BITS * jnp.minimum(lane, tiles - 1)), 0)
    slots = jnp.sum(slots, axis=1, keepdims=True)
    for i in range(len(blocks)):
        table[i] = slots[i, 0]


def band_columns(band, table, entries, places):
    rows = []
    for r in range(RB):
        tiles = []
        for entry, lead in zip(entries, places):
            for s in range(CB):
                slot = slot_of(table, entry, r * CB + s)
                start = pl.multiple_of(jnp.minimum(slot, CAP - 1) * TILE, TILE)
                tile = jnp.abs(band[(*lead, pl.ds(start, TILE), slice(None))])
                tiles.append(jnp.where(slot < CAP, tile, jnp.zeros_like(tile)))
        rows.append(jnp.concatenate(tiles, axis=1))
    return jnp.concatenate(rows, axis=0)


def spread_panel(panel, table, entry, core, owns):
    for z in range(2):
        for h, (dense, row) in enumerate(owns):
            owner = lax.rem(core + h, 2)
            for i in range(CB):
                for s in range(CB):
                    t = (owner * CB + i) * CB + s
                    at = row + (z * CB + i) * TILE
                    put_tile(dense, (at, s * TILE), panel, (z,), table, entry + z, t)


def sources(hi, y, ny, nl, js):
    for j in js:
        source = lax.rem(y - j + ny, ny)
        chips = (hi * ny + source, (1 - hi) * ny + source)
        yield chips, [(lax.div(chip, nl), lax.rem(chip, nl)) for chip in chips]


def all_blocks(band):
    return [(band, (x, k)) for x in range(band.shape[0]) for k in range(band.shape[1])]


def own_kernel(ny, js, place, mine, *rest):
    panels, (acc, spare, far_dense, heads, table, b_dense) = rest[:len(js)], rest[len(js):]
    hi, y, core = place[0], place[1], place[2]
    nl = mine.shape[1]
    blocks = all_blocks(mine)
    chips = len(blocks)
    blocks += [(panel, (z,)) for panel in panels for z in range(2)]
    read_slots(blocks, heads, table)
    for n, (entries, places) in enumerate(sources(hi, y, ny, nl, js)):
        spread_panel(panels[n], table, chips + 2 * n, core, ((b_dense, n * DEEP), (spare, n * DEEP)))
        columns = band_columns(mine, table, entries, places)
        part = jnp.dot(columns, b_dense[n * DEEP:(n + 1) * DEEP], preferred_element_type=jnp.float32)
        acc[...] = part if n == 0 else acc[...] + part
    ((entries, places),) = sources(hi, y, ny, nl, [ny // 2])
    far_dense[...] = band_columns(mine, table, entries, places)


def final_kernel(
    ny, js, place, keep, others, last, start, far_mine, spare, out, totals,
    heads, table, last_heads, last_table, b_dense, acc,
):
    hi, y, core = place[0], place[1], place[2]
    nl = others.shape[1]
    read_slots(all_blocks(others), heads, table)
    read_slots([(last, (z,)) for z in range(2)], last_heads, last_table)
    acc[...] = start[...]
    for n, (entries, places) in enumerate(sources(hi, y, ny, nl, js)):
        columns = band_columns(others, table, entries, places)
        acc[...] += jnp.dot(columns, spare[n * DEEP:(n + 1) * DEEP], preferred_element_type=jnp.float32)
    mine_rows, others_rows = b_dense.at[pl.ds(0, DEEP)], b_dense.at[pl.ds(DEEP, DEEP)]
    spread_panel(last, last_table, 0, core, ((mine_rows, 0), (others_rows, 0)))
    acc[...] += jnp.dot(far_mine[...], mine_rows[...], preferred_element_type=jnp.float32)
    ((entries, places),) = sources(hi, y, ny, nl, [ny // 2])
    columns = band_columns(others, table, entries, places)
    acc[...] += jnp.dot(columns, others_rows[...], preferred_element_type=jnp.float32)
    for s in range(CB):
        total = jnp.zeros((1, TILE), jnp.float32)
        for r in range(RB):
            at = (slice(r * TILE, (r + 1) * TILE), slice(s * TILE, (s + 1) * TILE))
            kept = acc[at] * keep[s, r].astype(jnp.float32)
            inflated = kept * kept
            out[at] = inflated
            total = total + jnp.sum(inflated, axis=0, keepdims=True)
        totals[:, s * TILE:(s + 1) * TILE] = total


def copies_kernel(line, out, sems):
    copies = [pltpu.make_async_copy(line, out.at[i], sems.at[i]) for i in range(out.shape[0])]
    for copy in copies:
        copy.start()
    for copy in copies:
        copy.wait()


def copies_of(line, count):
    return pl.pallas_call(
        copies_kernel,
        out_shape=jax.ShapeDtypeStruct((count, *line.shape), line.dtype),
        in_specs=[VMEM],
        out_specs=pl.BlockSpec(memory_space=pl.ANY),
        scratch_shapes=[pltpu.SemaphoreType.DMA((count,))],
        compiler_params=pltpu.CompilerParams(vmem_limit_bytes=8 * 2**20),
        name="line_copies",
    )(line)


def scratch(entries, *more):
    return [
        pltpu.VMEM((CAP, entries, TILE), jnp.float32),
        pltpu.SMEM((entries,), jnp.int32),
        *more,
    ]


def kernel_call(kernel, name, outs, smems, vmems, scratch_shapes):
    return pl.pallas_call(
        kernel,
        out_shape=outs,
        in_specs=[SMEM] * len(smems) + [VMEM] * len(vmems),
        out_specs=jax.tree.map(lambda _: VMEM, outs),
        scratch_shapes=scratch_shapes,
        compiler_params=pltpu.CompilerParams(vmem_limit_bytes=24 * 2**20),
        cost_estimate=pl.CostEstimate(flops=2**35, bytes_accessed=2**23, transcendentals=0),
        name=name,
    )(*smems, *vmems)


DEEP = 2 * CB * TILE
BLOCK_SUM = jax.ShapeDtypeStruct(BLOCK, jnp.float32)
FAR = jax.ShapeDtypeStruct((RB * TILE, DEEP), jnp.bfloat16)


def rows_of(count):
    return (count * DEEP, CB * TILE)


def own_part(ny, js, place, mine, panels):
    chips = mine.shape[0] * mine.shape[1]
    outs = (BLOCK_SUM, jax.ShapeDtypeStruct(rows_of(len(js)), jnp.bfloat16), FAR)
    shapes = scratch(
        chips + 2 * len(js),
        pltpu.VMEM(rows_of(len(js)), jnp.bfloat16),
    )
    return kernel_call(functools.partial(own_kernel, ny, js), "own_part", outs, [place], [mine, *panels], shapes)


def final_part(ny, js, place, keep, others, last, start, far_mine, spare):
    chips = others.shape[0] * others.shape[1]
    outs = (BLOCK_SUM, jax.ShapeDtypeStruct((1, CB * TILE), jnp.float32))
    shapes = scratch(chips) + scratch(
        2,
        pltpu.VMEM(rows_of(2), jnp.bfloat16),
        pltpu.VMEM(BLOCK, jnp.float32),
    )
    arrays = [others, last, start, far_mine, spare]
    return kernel_call(functools.partial(final_kernel, ny, js), "final_part", outs, [place, keep.T], arrays, shapes)


def again_kernel(block, out):
    out[...] = block[...]


def again(block):
    return pl.pallas_call(
        again_kernel,
        out_shape=jax.ShapeDtypeStruct(block.shape, block.dtype),
        in_specs=[VMEM],
        out_specs=VMEM,
        compiler_params=pltpu.CompilerParams(vmem_limit_bytes=4 * 2**20),
        cost_estimate=pl.CostEstimate(flops=2**36, bytes_accessed=2**20, transcendentals=0),
        name="both_again",
    )(block)


def shifted(array, axis, by):
    n = lax.axis_size(axis)
    return lax.ppermute(array, axis, [(i, (i + by) % n) for i in range(n)])


def body(matrix, in_pattern, out_pattern):
    ny, nx, nl = lax.axis_size("y"), lax.axis_size("x"), lax.axis_size("zl")
    packed = pack(matrix, in_pattern)
    other = shifted(packed, "zh", 1)
    line = lax.all_gather(packed, "zl", tiled=True)
    line, other = lax.optimization_barrier((line, other))
    own = jnp.concatenate([packed, other])
    mine = lax.all_to_all(copies_of(line, nx), "x", 0, 0)
    place = jnp.stack([lax.axis_index(a) for a in ("zh", "y", "core")])
    half = ny // 2
    panels = {0: own}
    for i in range(1, half):
        panels[i] = shifted(again(own) if i == 1 else panels[i - 1], "y", 1)
        panels[ny - i] = shifted(panels[(ny - i + 1) % ny], "y", -1)
    near = [j for j in range(ny) if j != half]
    sent, panels[half + 1] = lax.optimization_barrier((mine, panels[half + 1]))
    others = shifted(sent, "core", 1)
    last = shifted(panels[half + 1], "y", -1)
    start, spare, far_mine = own_part(ny, near, place, mine, [panels[j] for j in near])
    inflated, totals = final_part(ny, near, place, out_pattern, others, last, start, far_mine, spare)
    copies = jnp.broadcast_to(totals, (ny * lax.axis_size("zh"), totals.shape[1]))
    column_totals = jnp.sum(lax.all_to_all(copies, BLK, 0, 0, tiled=True), axis=0, keepdims=True)
    scaled = inflated / column_totals * float(SIZES[0] * SIZES[1] * RB * TILE)
    return jnp.maximum(scaled - prune_level, 0.0).astype(jnp.bfloat16)


def solution(mesh):
    fine = Mesh(mesh.devices.reshape(SIZES), AXES)
    spec = P(BLK, GRP)
    return jax.shard_map(body, mesh=fine, in_specs=(spec,) * 3, out_specs=spec, check_vma=False)
```

```python
import functools

import jax
import jax.numpy as jnp
from jax import lax
from jax.experimental import pallas as pl
from jax.experimental.pallas import tpu as pltpu
from jax.sharding import Mesh, PartitionSpec as P

prune_level = 0.5
TILE = 128
RB = 4
CB = 2
CAP = 4
HEAD = 16
SIGNS = 4
SLOT_BITS = 3
LEAST = 2.0**-126
PACK = CAP * TILE
AXES = ("zh", "y", "x", "zl", "core")
SIZES = (2, 8, 4, 4, 2)
BLK = ("zh", "y")
GRP = ("x", "zl", "core")


SMEM = pl.BlockSpec(memory_space=pltpu.SMEM)
VMEM = pl.BlockSpec(memory_space=pltpu.VMEM)
BLOCK = (RB * TILE, CB * TILE)


def pack_kernel(pattern_in, matrix_in, out, pattern, matrix, sems):
    pattern_copy = pltpu.make_async_copy(pattern_in, pattern, sems.at[0])
    matrix_copy = pltpu.make_async_copy(matrix_in, matrix, sems.at[1])
    matrix_copy.start()
    pattern_copy.start()
    lane = lax.broadcasted_iota(jnp.int32, (HEAD, TILE), 1)
    row = lax.broadcasted_iota(jnp.int32, (HEAD, TILE), 0)
    signs = (row == 0) & (lane < SIGNS)
    for slot in range(CAP):
        out[0, slot * TILE:slot * TILE + HEAD, :] = jnp.ones((HEAD, TILE), jnp.bfloat16)
    pattern_copy.wait()
    matrix_copy.wait()
    count = jnp.int32(0)
    for t in range(RB * CB):
        r, s = divmod(t, CB)
        present = pattern[s, r] != 0
        slot = jnp.minimum(count, CAP - 1)

        @pl.when(present)
        def _():
            place = pl.multiple_of(slot * TILE, TILE)
            tile = matrix[r * TILE:(r + 1) * TILE, s * TILE:(s + 1) * TILE]
            head = tile[:HEAD].astype(jnp.float32)
            size = jnp.maximum(head, LEAST)
            bit = lax.shift_right_logical(jnp.full_like(lane, t + RB * CB), jnp.minimum(lane, SIGNS)) & 1
            head = jnp.where(signs, jnp.where(bit == 1, -size, size), head)
            out[0, pl.ds(place, HEAD), :] = head.astype(jnp.bfloat16)
            out[0, pl.ds(pl.multiple_of(place + HEAD, HEAD), TILE - HEAD), :] = tile[HEAD:]

        count = count + present.astype(jnp.int32)


def pack(matrix, pattern):
    return pl.pallas_call(
        pack_kernel,
        out_shape=jax.ShapeDtypeStruct((1, PACK, TILE), jnp.bfloat16),
        in_specs=[pl.BlockSpec(memory_space=pl.ANY)] * 2,
        out_specs=VMEM,
        scratch_shapes=[
            pltpu.SMEM((CB, RB), jnp.int32),
            pltpu.VMEM(BLOCK, jnp.bfloat16),
            pltpu.SemaphoreType.DMA((2,)),
        ],
        name="pack_tiles",
    )(pattern.T, matrix)


def slot_of(table, row, t):
    return lax.shift_right_logical(table[row], SLOT_BITS * t) & (2**SLOT_BITS - 1)


def put_tile(dense, at, ref, lead, table, row, t):
    slot = slot_of(table, row, t)
    start = pl.multiple_of(jnp.minimum(slot, CAP - 1) * TILE, TILE)
    head = jnp.abs(ref[(*lead, pl.ds(start, HEAD), slice(None))])
    rest = ref[(*lead, pl.ds(pl.multiple_of(start + HEAD, HEAD), TILE - HEAD), slice(None))]
    r, c = at
    dense[r:r + HEAD, c:c + TILE] = jnp.where(slot < CAP, head, jnp.zeros_like(head))
    dense[r + HEAD:r + TILE, c:c + TILE] = jnp.where(slot < CAP, rest, jnp.zeros_like(rest))


def read_slots(blocks, heads, table):
    for i, (ref, lead) in enumerate(blocks):
        for slot in range(CAP):
            head = ref[(*lead, pl.ds(slot * TILE, HEAD), slice(None))].astype(jnp.float32)
            heads[slot, i:i + 1, :] = head[0:1]
    lane = lax.broadcasted_iota(jnp.int32, heads.shape[1:], 1)
    weight = jnp.where(lane < SIGNS, lax.shift_left(jnp.ones_like(lane), jnp.minimum(lane, SIGNS)), 0)
    slots = jnp.full(lane.shape, CAP, jnp.int32)
    for slot in range(CAP):
        code = jnp.sum(jnp.where(heads[slot] < 0, weight, 0), axis=1, keepdims=True)
        slots = jnp.where(code == lane + RB * CB, slot, slots)
    tiles = RB * CB
    slots = jnp.where(lane < tiles, lax.shift_left(slots, SLOT_BITS * jnp.minimum(lane, tiles - 1)), 0)
    slots = jnp.sum(slots, axis=1, keepdims=True)
    for i in range(len(blocks)):
        table[i] = slots[i, 0]


def band_columns(band, table, entries, places):
    rows = []
    for r in range(RB):
        tiles = []
        for entry, lead in zip(entries, places):
            for s in range(CB):
                slot = slot_of(table, entry, r * CB + s)
                start = pl.multiple_of(jnp.minimum(slot, CAP - 1) * TILE, TILE)
                tile = jnp.abs(band[(*lead, pl.ds(start, TILE), slice(None))])
                tiles.append(jnp.where(slot < CAP, tile, jnp.zeros_like(tile)))
        rows.append(jnp.concatenate(tiles, axis=1))
    return jnp.concatenate(rows, axis=0)


def spread_panel(panel, table, entry, core, owns):
    for z in range(2):
        for h, (dense, row) in enumerate(owns):
            owner = lax.rem(core + h, 2)
            for i in range(CB):
                for s in range(CB):
                    t = (owner * CB + i) * CB + s
                    at = row + (z * CB + i) * TILE
                    put_tile(dense, (at, s * TILE), panel, (z,), table, entry + z, t)


def sources(hi, y, ny, nl, js):
    for j in js:
        source = lax.rem(y - j + ny, ny)
        chips = (hi * ny + source, (1 - hi) * ny + source)
        yield chips, [(lax.div(chip, nl), lax.rem(chip, nl)) for chip in chips]


def all_blocks(band):
    return [(band, (x, k)) for x in range(band.shape[0]) for k in range(band.shape[1])]


def own_kernel(ny, js, place, mine, *rest):
    panels, (acc, spare, far_dense, heads, table, b_dense) = rest[:len(js)], rest[len(js):]
    hi, y, core = place[0], place[1], place[2]
    nl = mine.shape[1]
    blocks = all_blocks(mine)
    chips = len(blocks)
    blocks += [(panel, (z,)) for panel in panels for z in range(2)]
    read_slots(blocks, heads, table)
    for n, (entries, places) in enumerate(sources(hi, y, ny, nl, js)):
        spread_panel(panels[n], table, chips + 2 * n, core, ((b_dense, n * DEEP), (spare, n * DEEP)))
        columns = band_columns(mine, table, entries, places)
        part = jnp.dot(columns, b_dense[n * DEEP:(n + 1) * DEEP], preferred_element_type=jnp.float32)
        acc[...] = part if n == 0 else acc[...] + part
    ((entries, places),) = sources(hi, y, ny, nl, [ny // 2])
    far_dense[...] = band_columns(mine, table, entries, places)


def final_kernel(
    ny, js, place, keep, others, last, start, far_mine, spare, out, totals,
    heads, table, last_heads, last_table, b_dense, acc,
):
    hi, y, core = place[0], place[1], place[2]
    nl = others.shape[1]
    read_slots(all_blocks(others), heads, table)
    read_slots([(last, (z,)) for z in range(2)], last_heads, last_table)
    acc[...] = start[...]
    for n, (entries, places) in enumerate(sources(hi, y, ny, nl, js)):
        columns = band_columns(others, table, entries, places)
        acc[...] += jnp.dot(columns, spare[n * DEEP:(n + 1) * DEEP], preferred_element_type=jnp.float32)
    mine_rows, others_rows = b_dense.at[pl.ds(0, DEEP)], b_dense.at[pl.ds(DEEP, DEEP)]
    spread_panel(last, last_table, 0, core, ((mine_rows, 0), (others_rows, 0)))
    acc[...] += jnp.dot(far_mine[...], mine_rows[...], preferred_element_type=jnp.float32)
    ((entries, places),) = sources(hi, y, ny, nl, [ny // 2])
    columns = band_columns(others, table, entries, places)
    acc[...] += jnp.dot(columns, others_rows[...], preferred_element_type=jnp.float32)
    for s in range(CB):
        total = jnp.zeros((1, TILE), jnp.float32)
        for r in range(RB):
            at = (slice(r * TILE, (r + 1) * TILE), slice(s * TILE, (s + 1) * TILE))
            kept = acc[at] * keep[s, r].astype(jnp.float32)
            inflated = kept * kept
            out[at] = inflated
            total = total + jnp.sum(inflated, axis=0, keepdims=True)
        totals[:, s * TILE:(s + 1) * TILE] = total


def copies_kernel(line, out, sems):
    copies = [pltpu.make_async_copy(line, out.at[i], sems.at[i]) for i in range(out.shape[0])]
    for copy in copies:
        copy.start()
    for copy in copies:
        copy.wait()


def copies_of(line, count):
    return pl.pallas_call(
        copies_kernel,
        out_shape=jax.ShapeDtypeStruct((count, *line.shape), line.dtype),
        in_specs=[VMEM],
        out_specs=pl.BlockSpec(memory_space=pl.ANY),
        scratch_shapes=[pltpu.SemaphoreType.DMA((count,))],
        compiler_params=pltpu.CompilerParams(vmem_limit_bytes=8 * 2**20),
        name="line_copies",
    )(line)


def scratch(entries, *more):
    return [
        pltpu.VMEM((CAP, entries, TILE), jnp.float32),
        pltpu.SMEM((entries,), jnp.int32),
        *more,
    ]


def kernel_call(kernel, name, outs, smems, vmems, scratch_shapes):
    return pl.pallas_call(
        kernel,
        out_shape=outs,
        in_specs=[SMEM] * len(smems) + [VMEM] * len(vmems),
        out_specs=jax.tree.map(lambda _: VMEM, outs),
        scratch_shapes=scratch_shapes,
        compiler_params=pltpu.CompilerParams(vmem_limit_bytes=24 * 2**20),
        cost_estimate=pl.CostEstimate(flops=2**35, bytes_accessed=2**23, transcendentals=0),
        name=name,
    )(*smems, *vmems)


DEEP = 2 * CB * TILE
BLOCK_SUM = jax.ShapeDtypeStruct(BLOCK, jnp.float32)
FAR = jax.ShapeDtypeStruct((RB * TILE, DEEP), jnp.bfloat16)


def rows_of(count):
    return (count * DEEP, CB * TILE)


def own_part(ny, js, place, mine, panels):
    chips = mine.shape[0] * mine.shape[1]
    outs = (BLOCK_SUM, jax.ShapeDtypeStruct(rows_of(len(js)), jnp.bfloat16), FAR)
    shapes = scratch(
        chips + 2 * len(js),
        pltpu.VMEM(rows_of(len(js)), jnp.bfloat16),
    )
    return kernel_call(functools.partial(own_kernel, ny, js), "own_part", outs, [place], [mine, *panels], shapes)


def final_part(ny, js, place, keep, others, last, start, far_mine, spare):
    chips = others.shape[0] * others.shape[1]
    outs = (BLOCK_SUM, jax.ShapeDtypeStruct((1, CB * TILE), jnp.float32))
    shapes = scratch(chips) + scratch(
        2,
        pltpu.VMEM(rows_of(2), jnp.bfloat16),
        pltpu.VMEM(BLOCK, jnp.float32),
    )
    arrays = [others, last, start, far_mine, spare]
    return kernel_call(functools.partial(final_kernel, ny, js), "final_part", outs, [place, keep.T], arrays, shapes)


def again_kernel(block, out):
    out[...] = block[...]


def again(block):
    return pl.pallas_call(
        again_kernel,
        out_shape=jax.ShapeDtypeStruct(block.shape, block.dtype),
        in_specs=[VMEM],
        out_specs=VMEM,
        compiler_params=pltpu.CompilerParams(vmem_limit_bytes=4 * 2**20),
        cost_estimate=pl.CostEstimate(flops=2**36, bytes_accessed=2**20, transcendentals=0),
        name="both_again",
    )(block)


def shifted(array, axis, by):
    n = lax.axis_size(axis)
    return lax.ppermute(array, axis, [(i, (i + by) % n) for i in range(n)])


def body(matrix, in_pattern, out_pattern):
    ny, nx, nl = lax.axis_size("y"), lax.axis_size("x"), lax.axis_size("zl")
    packed = pack(matrix, in_pattern)
    other = shifted(packed, "zh", 1)
    line = lax.all_gather(packed, "zl", tiled=True)
    line, other = lax.optimization_barrier((line, other))
    own = jnp.concatenate([packed, other])
    mine = lax.all_to_all(copies_of(line, nx), "x", 0, 0)
    place = jnp.stack([lax.axis_index(a) for a in ("zh", "y", "core")])
    half = ny // 2
    panels = {0: own}
    for i in range(1, half):
        panels[i] = shifted(again(own) if i == 1 else panels[i - 1], "y", 1)
        panels[ny - i] = shifted(panels[(ny - i + 1) % ny], "y", -1)
    near = [j for j in range(ny) if j != half]
    sent, panels[half + 1] = lax.optimization_barrier((mine, panels[half + 1]))
    others = shifted(sent, "core", 1)
    last = shifted(panels[half + 1], "y", -1)
    start, spare, far_mine = own_part(ny, near, place, mine, [panels[j] for j in near])
    inflated, totals = final_part(ny, near, place, out_pattern, others, last, start, far_mine, spare)
    copies = jnp.broadcast_to(totals, (ny * lax.axis_size("zh"), totals.shape[1]))
    column_totals = jnp.sum(lax.all_to_all(copies, ("y", "zh"), 0, 0, tiled=True), axis=0, keepdims=True)
    scaled = inflated / column_totals * float(SIZES[0] * SIZES[1] * RB * TILE)
    return jnp.maximum(scaled - prune_level, 0.0).astype(jnp.bfloat16)


def solution(mesh):
    fine = Mesh(mesh.devices.reshape(SIZES), AXES)
    spec = P(BLK, GRP)
    return jax.shard_map(body, mesh=fine, in_specs=(spec,) * 3, out_specs=spec, check_vma=False)
```
